768 devices in a mesh: row: 16 (over y_lo, x, core), col: 48 (over z, y_hi).
Axes of the slice: x: 4, y: 8 (y_hi: 4, y_lo: 2; y = y_hi * 2 + y_lo), z: 12, core: 2. Of those that a mesh axis runs over, the one named last changes fastest.
Arguments:
- values: bfloat16 [6144, 6144], P('row', 'col'), may hold values from -6 to 6
- occupancy: int32 [48, 48], P('row', 'col'), may hold values 0 or 1
Outputs:
- square_slab: bfloat16 [4096, 6144], P('row', 'col')
- sign_step: bfloat16 [4096, 6144], P('row', 'col')
The draws below stay inside these ranges and needn't reach their ends.
All inputs are finite; a program needn't handle non-finite values. No bound on the sum of `occupancy` on one device may be relied on, other than what follows from the above.
Results may differ from the reference program's by a relative error of at most 0.0015.
Values may be sent and summed in bfloat16 or wider, within the bound.
No kernel may reach another device: no remote copies, remote signals or barrier semaphores. Data moves between devices by JAX's collectives and lax.ppermute only.
A program may use at most 32 MiB of HBM per device.

```python
import math
import jax
import jax.numpy as jnp

BS = 128
SLAB = 256
NB = 48
ORDER = 6144
RD = 384
N_ROW = 16


def set_ends(result, key, smallest, high):
    extent = result.shape
    index_at = [jax.random.randint(jax.random.fold_in(key, axis), (), 0, extent[axis]) for axis in range(len(extent))]
    result = result.at[tuple(index_at)].set(smallest)
    longest = extent.index(max(extent))
    index_at[longest] = (index_at[longest] + 1) % extent[longest]
    return result.at[tuple(index_at)].set(high)


def block_levels(key, shape, split, least, largest):
    gain, own = 1.0, jax.random.fold_in(key, 6)
    for axis_at, shards_of in split:
        draws = jnp.exp(jax.random.uniform(jax.random.fold_in(own, axis_at), (shards_of,), jnp.float32, least / len(split), largest / len(split)))
        gain = gain * jnp.repeat(draws, shape[axis_at] // shards_of).reshape([-1 if axis == axis_at else 1 for axis in range(len(shape))])
    return gain


def noise(stream_key, shape, width, most, shards=(), dtype=jnp.bfloat16):
    values = width * jax.random.normal(stream_key, shape, jnp.float32)
    if shards:
        values = values * block_levels(stream_key, shape, shards, -0.22, 0.18)
    return jnp.clip(values, -most, most).astype(dtype)


def setup_inputs(seed: int = 0) -> dict:
    streams_of = jax.random.split(jax.random.key(seed), 3)
    return {
        "values": noise(streams_of[0], (ORDER, ORDER), 1.0, 6.0, ((0, 16), (1, 48))),
        "occupancy": set_ends((jax.random.randint(streams_of[1], (NB, NB), 0, 2) < 1).astype(jnp.int32), jax.random.fold_in(streams_of[1], 1), 0, 1),
    }


def expand_blocks(occupancy):
    return jnp.repeat(jnp.repeat(occupancy, BS, 0), BS, 1).astype(jnp.float32)

def slab_rows(array):
    return array.reshape(N_ROW, RD, ORDER)[:, :SLAB].reshape(N_ROW * SLAB, ORDER)

def reference(values, occupancy):
    block_mask = expand_blocks(occupancy)
    matrix = (values.astype(jnp.float32) * block_mask).astype(jnp.bfloat16)
    slab = slab_rows(matrix)
    slab_mask = slab_rows(block_mask)
    factor = 1.0 / math.sqrt(ORDER)
    first_sum = jnp.dot(slab, matrix, preferred_element_type=jnp.float32)
    square_slab = (first_sum * factor * slab_mask).astype(jnp.bfloat16)
    second_sum = jnp.dot(square_slab, matrix, preferred_element_type=jnp.float32)
    sign_step = ((1.5 * slab.astype(jnp.float32) - 0.5 * factor * second_sum) * slab_mask).astype(jnp.bfloat16)
    return (square_slab, sign_step)
```

```python
import math

import jax
import jax.numpy as jnp
from jax import lax
from jax.experimental import pallas as pl
from jax.experimental.pallas import tpu as pltpu
from jax.sharding import Mesh
from jax.sharding import PartitionSpec as P

BS = 128
SLAB = 256
ORDER = 6144
FACTOR = 1.0 / math.sqrt(ORDER)
N_YL, N_X, N_CORE, N_Z, N_YH = 2, 4, 2, 12, 4
LIMIT = 24 * 1024 * 1024


def vmem(n):
    return [pl.BlockSpec(memory_space=pltpu.VMEM)] * n


def smem(n):
    return [pl.BlockSpec(memory_space=pltpu.SMEM)] * n


def position():
    yl, x, core = lax.axis_index("yl"), lax.axis_index("x"), lax.axis_index("core")
    return jnp.stack([(yl * N_X + x) * N_CORE + core, core, lax.axis_index("yh")])


def prepare(pos_ref, occ_ref, values_ref, slab_ref, send_ref):
    for t in range(2):
        rows = pl.ds(t * BS, BS)
        slab_ref[rows, :] = values_ref[rows, :] * occ_ref[t].astype(jnp.float32).astype(jnp.bfloat16)
    first = 3 * pos_ref[0]
    for q in range(N_YH):
        t = lax.rem(q + 4 * 48 - first, 4)
        held = jnp.minimum(t, 2)
        keep = jnp.where(t < 3, occ_ref[held], 0).astype(jnp.float32).astype(jnp.bfloat16)
        block = values_ref[pl.ds(pl.multiple_of(held * BS, BS), BS), :] * keep
        for j in range(N_YL * N_X):
            send_ref[j * N_YH + q] = block


def assemble(s_ref, sk_ref):
    for z in range(N_Z):
        sk_ref[:, z * BS:(z + 1) * BS] = s_ref[z]


def first_product(pos_ref, s_ref, mine_ref, other_ref, out_ref, mk_ref, sk_ref):
    assemble(s_ref, sk_ref)
    my_core, yh = pos_ref[1], pos_ref[2]
    for z in range(N_Z):
        r = lax.div(4 * z + yh, 3)
        slot = lax.div(r, 2) * N_YH
        here = lax.rem(r, 2) == my_core

        @pl.when(here)
        def _():
            for q in range(N_YH):
                mk_ref[z * BS:(z + 1) * BS, q * BS:(q + 1) * BS] = mine_ref[slot + q]

        @pl.when(jnp.logical_not(here))
        def _():
            for q in range(N_YH):
                mk_ref[z * BS:(z + 1) * BS, q * BS:(q + 1) * BS] = other_ref[slot + q]

    total = jnp.dot(sk_ref[...], mk_ref[...], preferred_element_type=jnp.float32)
    for q in range(N_YH):
        out_ref[q] = total[:, q * BS:(q + 1) * BS]


def second_product(s_ref, mk_ref, out_ref, sk_ref):
    assemble(s_ref, sk_ref)
    total = jnp.dot(sk_ref[...], mk_ref[...], preferred_element_type=jnp.float32)
    for q in range(N_YH):
        out_ref[q] = total[:, q * BS:(q + 1) * BS]


def finish_square(occ_ref, parts_ref, out_ref):
    for t in range(2):
        rows = pl.ds(t * BS, BS)
        total = (parts_ref[0, rows, :] + parts_ref[1, rows, :]) + (parts_ref[2, rows, :] + parts_ref[3, rows, :])
        out_ref[rows, :] = (total * FACTOR * occ_ref[t].astype(jnp.float32)).astype(jnp.bfloat16)


def finish_sign(occ_ref, slab_ref, parts_ref, out_ref):
    for t in range(2):
        rows = pl.ds(t * BS, BS)
        total = (parts_ref[0, rows, :] + parts_ref[1, rows, :]) + (parts_ref[2, rows, :] + parts_ref[3, rows, :])
        step = 1.5 * slab_ref[rows, :].astype(jnp.float32) - 0.5 * FACTOR * total
        out_ref[rows, :] = (step * occ_ref[t].astype(jnp.float32)).astype(jnp.bfloat16)


def shape(*dims, dtype=jnp.bfloat16):
    return jax.ShapeDtypeStruct(dims, dtype)


def kernel(body, n_smem, n_vmem, out_shape, scratch=(), flops=0, moved=1 << 20):
    return pl.pallas_call(
        body,
        out_shape=out_shape,
        in_specs=smem(n_smem) + vmem(n_vmem),
        out_specs=jax.tree.map(lambda _: pl.BlockSpec(memory_space=pltpu.VMEM), out_shape),
        scratch_shapes=list(scratch),
        compiler_params=pltpu.CompilerParams(vmem_limit_bytes=LIMIT),
        cost_estimate=pl.CostEstimate(flops=flops, bytes_accessed=moved, transcendentals=0),
    )


def local(values, occupancy):
    occ = occupancy.reshape(3)
    pos = position()
    group = N_YL * N_X * N_YH
    slab, send = kernel(prepare, 2, 1, (shape(SLAB, BS), shape(group, BS, BS)))(pos, occ, values)
    mine = lax.all_to_all(send, ("yl", "x", "yh"), 0, 0, tiled=True)
    other = lax.ppermute(mine, "core", [(0, 1), (1, 0)])
    gathered = lax.all_gather(slab, "z", axis=0, tiled=False)
    cost = dict(flops=2 * SLAB * 12 * BS * 4 * BS, moved=4 << 20)
    sk = pltpu.VMEM((SLAB, N_Z * BS), jnp.bfloat16)
    parts_shape = shape(N_YH, SLAB, BS, dtype=jnp.float32)
    parts, mk = kernel(
        first_product, 1, 3, (parts_shape, shape(N_Z * BS, N_YH * BS)), (sk,), **cost
    )(pos, gathered, mine, other)
    parts = lax.all_to_all(parts, "yh", 0, 0, tiled=True)
    square_slab = kernel(finish_square, 1, 1, shape(SLAB, BS))(occ, parts)
    gathered = lax.all_gather(square_slab, "z", axis=0, tiled=False)
    parts = kernel(second_product, 0, 2, parts_shape, (sk,), **cost)(gathered, mk)
    parts = lax.all_to_all(parts, "yh", 0, 0, tiled=True)
    sign_step = kernel(finish_sign, 1, 2, shape(SLAB, BS))(occ, slab, parts)
    return (square_slab, sign_step)


def solution(mesh):
    fine = Mesh(
        mesh.devices.reshape(N_YL, N_X, N_CORE, N_Z, N_YH), ("yl", "x", "core", "z", "yh")
    )
    spec = P(("yl", "x", "core"), ("z", "yh"))
    return jax.shard_map(local, mesh=fine, in_specs=(spec, spec), out_specs=(spec, spec), check_vma=False)
```

```python
import math

import jax
import jax.numpy as jnp
from jax import lax
from jax.experimental import pallas as pl
from jax.experimental.pallas import tpu as pltpu
from jax.sharding import Mesh
from jax.sharding import PartitionSpec as P

BS = 128
SLAB = 256
ORDER = 6144
FACTOR = 1.0 / math.sqrt(ORDER)
N_YL, N_X, N_CORE, N_Z, N_YH = 2, 4, 2, 12, 4
LIMIT = 24 * 1024 * 1024


def vmem(n):
    return [pl.BlockSpec(memory_space=pltpu.VMEM)] * n


def smem(n):
    return [pl.BlockSpec(memory_space=pltpu.SMEM)] * n


def position():
    yl, x, core = lax.axis_index("yl"), lax.axis_index("x"), lax.axis_index("core")
    return jnp.stack([(yl * N_X + x) * N_CORE + core, core, lax.axis_index("yh")])


def prepare(pos_ref, occ_ref, values_ref, slab_ref, send_ref):
    for t in range(2):
        rows = pl.ds(t * BS, BS)
        slab_ref[rows, :] = values_ref[rows, :] * occ_ref[t].astype(jnp.float32).astype(jnp.bfloat16)
    first = 3 * pos_ref[0]
    for q in range(N_YH):
        t = lax.rem(q + 4 * 48 - first, 4)
        held = jnp.minimum(t, 2)
        keep = jnp.where(t < 3, occ_ref[held], 0).astype(jnp.float32).astype(jnp.bfloat16)
        block = values_ref[pl.ds(pl.multiple_of(held * BS, BS), BS), :] * keep
        for j in range(N_YL * N_X):
            send_ref[j * N_YH + q] = block


def assemble(s_ref, sk_ref):
    for z in range(N_Z):
        sk_ref[:, z * BS:(z + 1) * BS] = s_ref[z]


def first_product(pos_ref, s_ref, mine_ref, other_ref, out_ref, mk_ref, sk_ref):
    assemble(s_ref, sk_ref)
    my_core, yh = pos_ref[1], pos_ref[2]
    for z in range(N_Z):
        r = lax.div(4 * z + yh, 3)
        slot = lax.div(r, 2) * N_YH
        here = lax.rem(r, 2) == my_core

        @pl.when(here)
        def _():
            for q in range(N_YH):
                mk_ref[z * BS:(z + 1) * BS, q * BS:(q + 1) * BS] = mine_ref[slot + q]

        @pl.when(jnp.logical_not(here))
        def _():
            for q in range(N_YH):
                mk_ref[z * BS:(z + 1) * BS, q * BS:(q + 1) * BS] = other_ref[slot + q]

    total = jnp.dot(sk_ref[...], mk_ref[...], preferred_element_type=jnp.float32)
    for q in range(N_YH):
        out_ref[q] = total[:, q * BS:(q + 1) * BS]


def second_product(s_ref, mk_ref, out_ref, sk_ref):
    assemble(s_ref, sk_ref)
    total = jnp.dot(sk_ref[...], mk_ref[...], preferred_element_type=jnp.float32)
    for q in range(N_YH):
        out_ref[q] = total[:, q * BS:(q + 1) * BS]


def finish_square(occ_ref, parts_ref, out_ref):
    for t in range(2):
        rows = pl.ds(t * BS, BS)
        total = (parts_ref[0, rows, :] + parts_ref[1, rows, :]) + (parts_ref[2, rows, :] + parts_ref[3, rows, :])
        out_ref[rows, :] = (total * FACTOR * occ_ref[t].astype(jnp.float32)).astype(jnp.bfloat16)


def finish_sign(occ_ref, slab_ref, parts_ref, out_ref):
    for t in range(2):
        rows = pl.ds(t * BS, BS)
        total = (parts_ref[0, rows, :] + parts_ref[1, rows, :]) + (parts_ref[2, rows, :] + parts_ref[3, rows, :])
        step = 1.5 * slab_ref[rows, :].astype(jnp.float32) - 0.5 * FACTOR * total
        out_ref[rows, :] = (step * occ_ref[t].astype(jnp.float32)).astype(jnp.bfloat16)


def shape(*dims, dtype=jnp.bfloat16):
    return jax.ShapeDtypeStruct(dims, dtype)


def kernel(body, n_smem, n_vmem, out_shape, scratch=(), flops=0, moved=1 << 20):
    return pl.pallas_call(
        body,
        out_shape=out_shape,
        in_specs=smem(n_smem) + vmem(n_vmem),
        out_specs=jax.tree.map(lambda _: pl.BlockSpec(memory_space=pltpu.VMEM), out_shape),
        scratch_shapes=list(scratch),
        compiler_params=pltpu.CompilerParams(vmem_limit_bytes=LIMIT),
        cost_estimate=pl.CostEstimate(flops=flops, bytes_accessed=moved, transcendentals=0),
    )


def local(values, occupancy):
    occ = occupancy.reshape(3)
    pos = position()
    group = N_YL * N_X * N_YH
    slab, send = kernel(prepare, 2, 1, (shape(SLAB, BS), shape(group, BS, BS)))(pos, occ, values)
    mine = lax.all_to_all(send, ("yl", "x", "yh"), 0, 0, tiled=True)
    gathered = lax.all_gather(slab, "z", axis=0, tiled=False)
    mine, gathered = lax.optimization_barrier((mine, gathered))
    other = lax.ppermute(mine, "core", [(0, 1), (1, 0)])
    cost = dict(flops=2 * SLAB * 12 * BS * 4 * BS, moved=4 << 20)
    sk = pltpu.VMEM((SLAB, N_Z * BS), jnp.bfloat16)
    parts_shape = shape(N_YH, SLAB, BS, dtype=jnp.float32)
    parts, mk = kernel(
        first_product, 1, 3, (parts_shape, shape(N_Z * BS, N_YH * BS)), (sk,), **cost
    )(pos, gathered, mine, other)
    parts = lax.all_to_all(parts, "yh", 0, 0, tiled=True)
    square_slab = kernel(finish_square, 1, 1, shape(SLAB, BS))(occ, parts)
    gathered = lax.all_gather(square_slab, "z", axis=0, tiled=False)
    parts = kernel(second_product, 0, 2, parts_shape, (sk,), **cost)(gathered, mk)
    parts = lax.all_to_all(parts, "yh", 0, 0, tiled=True)
    sign_step = kernel(finish_sign, 1, 2, shape(SLAB, BS))(occ, slab, parts)
    return (square_slab, sign_step)


def solution(mesh):
    fine = Mesh(
        mesh.devices.reshape(N_YL, N_X, N_CORE, N_Z, N_YH), ("yl", "x", "core", "z", "yh")
    )
    spec = P(("yl", "x", "core"), ("z", "yh"))
    return jax.shard_map(local, mesh=fine, in_specs=(spec, spec), out_specs=(spec, spec), check_vma=False)
```

```python
import math

import jax
import jax.numpy as jnp
from jax import lax
from jax.experimental import pallas as pl
from jax.experimental.pallas import tpu as pltpu
from jax.sharding import Mesh
from jax.sharding import PartitionSpec as P

BS = 128
SLAB = 256
ORDER = 6144
FACTOR = 1.0 / math.sqrt(ORDER)
N_YL, N_X, N_CORE, N_Z, N_YH = 2, 4, 2, 12, 4
LIMIT = 24 * 1024 * 1024


def vmem(n):
    return [pl.BlockSpec(memory_space=pltpu.VMEM)] * n


def row_index():
    return (lax.axis_index("yl") * N_X + lax.axis_index("x")) * N_CORE + lax.axis_index("core")


def prepare(occ_hbm, values_hbm, slab_ref, mask_ref, send_hbm, occ_ref, values_ref, blocks_ref, in_sem, out_sem):
    copies = [
        pltpu.make_async_copy(occ_hbm, occ_ref, in_sem.at[0]),
        pltpu.make_async_copy(values_hbm, values_ref, in_sem.at[1]),
    ]
    for copy in copies:
        copy.start()
    for copy in copies:
        copy.wait()
    first = 3 * row_index()
    for q in range(N_YH):
        t = lax.rem(q + 4 * 48 - first, 4)
        held = jnp.minimum(t, 2)
        keep = jnp.where(t < 3, occ_ref[held], 0).astype(jnp.float32).astype(jnp.bfloat16)
        blocks_ref[q] = values_ref[pl.ds(pl.multiple_of(held * BS, BS), BS), :] * keep
    copies = [
        pltpu.make_async_copy(blocks_ref, send_hbm.at[pl.ds(j * N_YH, N_YH)], out_sem.at[j])
        for j in range(N_YL * N_X)
    ]
    for copy in copies:
        copy.start()
    for t in range(2):
        rows = pl.ds(t * BS, BS)
        keep = occ_ref[t].astype(jnp.float32)
        slab_ref[rows, :] = values_ref[rows, :] * keep.astype(jnp.bfloat16)
        mask_ref[t * 8:(t + 1) * 8, :] = jnp.full((8, BS), keep, jnp.float32)
    for copy in copies:
        copy.wait()


def assemble(s_ref, sk_ref):
    for z in range(N_Z):
        sk_ref[:, z * BS:(z + 1) * BS] = s_ref[z]


def first_product(s_ref, mine_ref, other_ref, out_ref, mk_ref, sk_ref):
    assemble(s_ref, sk_ref)
    my_core, yh = lax.axis_index("core"), lax.axis_index("yh")
    for z in range(N_Z):
        r = lax.div(4 * z + yh, 3)
        slot = lax.div(r, 2) * N_YH
        here = lax.rem(r, 2) == my_core

        @pl.when(here)
        def _():
            for q in range(N_YH):
                mk_ref[z * BS:(z + 1) * BS, q * BS:(q + 1) * BS] = mine_ref[slot + q]

        @pl.when(jnp.logical_not(here))
        def _():
            for q in range(N_YH):
                mk_ref[z * BS:(z + 1) * BS, q * BS:(q + 1) * BS] = other_ref[slot + q]

    total = jnp.dot(sk_ref[...], mk_ref[...], preferred_element_type=jnp.float32)
    for q in range(N_YH):
        out_ref[q] = total[:, q * BS:(q + 1) * BS]


def second_product(s_ref, mk_ref, out_ref, sk_ref):
    assemble(s_ref, sk_ref)
    total = jnp.dot(sk_ref[...], mk_ref[...], preferred_element_type=jnp.float32)
    for q in range(N_YH):
        out_ref[q] = total[:, q * BS:(q + 1) * BS]


def finish_square(mask_ref, parts_ref, out_ref):
    for t in range(2):
        rows = pl.ds(t * BS, BS)
        total = (parts_ref[0, rows, :] + parts_ref[1, rows, :]) + (parts_ref[2, rows, :] + parts_ref[3, rows, :])
        out_ref[rows, :] = (total * FACTOR * mask_ref[t * 8:t * 8 + 1, :]).astype(jnp.bfloat16)


def finish_sign(mask_ref, slab_ref, parts_ref, out_ref):
    for t in range(2):
        rows = pl.ds(t * BS, BS)
        total = (parts_ref[0, rows, :] + parts_ref[1, rows, :]) + (parts_ref[2, rows, :] + parts_ref[3, rows, :])
        step = 1.5 * slab_ref[rows, :].astype(jnp.float32) - 0.5 * FACTOR * total
        out_ref[rows, :] = (step * mask_ref[t * 8:t * 8 + 1, :]).astype(jnp.bfloat16)


def shape(*dims, dtype=jnp.bfloat16):
    return jax.ShapeDtypeStruct(dims, dtype)


def kernel(body, n_in, out_shape, scratch=(), flops=0, moved=1 << 20):
    return pl.pallas_call(
        body,
        out_shape=out_shape,
        in_specs=vmem(n_in),
        out_specs=jax.tree.map(lambda _: pl.BlockSpec(memory_space=pltpu.VMEM), out_shape),
        scratch_shapes=list(scratch),
        compiler_params=pltpu.CompilerParams(vmem_limit_bytes=LIMIT),
        cost_estimate=pl.CostEstimate(flops=flops, bytes_accessed=moved, transcendentals=0),
    )


def local(values, occupancy):
    group = N_YL * N_X * N_YH
    anywhere, in_vmem = pl.BlockSpec(memory_space=pl.ANY), pl.BlockSpec(memory_space=pltpu.VMEM)
    slab, mask, send = pl.pallas_call(
        prepare,
        out_shape=(shape(SLAB, BS), shape(16, BS, dtype=jnp.float32), shape(group, BS, BS)),
        in_specs=[anywhere, anywhere],
        out_specs=(in_vmem, in_vmem, anywhere),
        scratch_shapes=[
            pltpu.SMEM((3,), jnp.int32),
            pltpu.VMEM((3 * BS, BS), jnp.bfloat16),
            pltpu.VMEM((N_YH, BS, BS), jnp.bfloat16),
            pltpu.SemaphoreType.DMA((2,)),
            pltpu.SemaphoreType.DMA((N_YL * N_X,)),
        ],
        compiler_params=pltpu.CompilerParams(vmem_limit_bytes=60 * 1024 * 1024),
    )(occupancy.reshape(3), values)
    mine = lax.all_to_all(send, ("yl", "x", "yh"), 0, 0, tiled=True)
    gathered = lax.all_gather(slab, "z", axis=0, tiled=False)
    mine, gathered = lax.optimization_barrier((mine, gathered))
    other = lax.ppermute(mine, "core", [(0, 1), (1, 0)])
    cost = dict(flops=2 * SLAB * 12 * BS * 4 * BS, moved=4 << 20)
    sk = pltpu.VMEM((SLAB, N_Z * BS), jnp.bfloat16)
    parts_shape = shape(N_YH, SLAB, BS, dtype=jnp.float32)
    parts, mk = kernel(
        first_product, 3, (parts_shape, shape(N_Z * BS, N_YH * BS)), (sk,), **cost
    )(gathered, mine, other)
    parts = lax.all_to_all(parts, "yh", 0, 0, tiled=True)
    square_slab = kernel(finish_square, 2, shape(SLAB, BS))(mask, parts)
    gathered = lax.all_gather(square_slab, "z", axis=0, tiled=False)
    parts = kernel(second_product, 2, parts_shape, (sk,), **cost)(gathered, mk)
    parts = lax.all_to_all(parts, "yh", 0, 0, tiled=True)
    sign_step = kernel(finish_sign, 3, shape(SLAB, BS))(mask, slab, parts)
    return (square_slab, sign_step)


def solution(mesh):
    fine = Mesh(
        mesh.devices.reshape(N_YL, N_X, N_CORE, N_Z, N_YH), ("yl", "x", "core", "z", "yh")
    )
    spec = P(("yl", "x", "core"), ("z", "yh"))
    return jax.shard_map(local, mesh=fine, in_specs=(spec, spec), out_specs=(spec, spec), check_vma=False)
```

```python
import math

import jax
import jax.numpy as jnp
from jax import lax
from jax.experimental import pallas as pl
from jax.experimental.pallas import tpu as pltpu
from jax.sharding import Mesh
from jax.sharding import PartitionSpec as P

BS = 128
SLAB = 256
ORDER = 6144
FACTOR = 1.0 / math.sqrt(ORDER)
N_YL, N_X, N_CORE, N_Z, N_YH = 2, 4, 2, 12, 4
N_GROUP = SLAB // 16
LIMIT = 24 * 1024 * 1024


def vmem(n):
    return [pl.BlockSpec(memory_space=pltpu.VMEM)] * n


def row_index():
    return (lax.axis_index("yl") * N_X + lax.axis_index("x")) * N_CORE + lax.axis_index("core")


def prepare(occ_hbm, values_hbm, slab_ref, mask_ref, send_hbm, occ_ref, values_ref, blocks_ref, in_sem, out_sem):
    copies = [
        pltpu.make_async_copy(occ_hbm, occ_ref, in_sem.at[0]),
        pltpu.make_async_copy(values_hbm, values_ref, in_sem.at[1]),
    ]
    for copy in copies:
        copy.start()
    for copy in copies:
        copy.wait()
    first = 3 * row_index()
    for q in range(N_YH):
        t = lax.rem(q + 4 * 48 - first, 4)
        held = jnp.minimum(t, 2)
        keep = jnp.where(t < 3, occ_ref[held], 0).astype(jnp.float32).astype(jnp.bfloat16)
        blocks_ref[q] = values_ref[pl.ds(pl.multiple_of(held * BS, BS), BS), :] * keep
    copies = [
        pltpu.make_async_copy(blocks_ref, send_hbm.at[pl.ds(j * N_YH, N_YH)], out_sem.at[j])
        for j in range(N_YL * N_X)
    ]
    for copy in copies:
        copy.start()
    for t in range(2):
        rows = pl.ds(t * BS, BS)
        keep = occ_ref[t].astype(jnp.float32)
        slab_ref[rows, :] = values_ref[rows, :] * keep.astype(jnp.bfloat16)
        mask_ref[t * 8:(t + 1) * 8, :] = jnp.full((8, BS), keep, jnp.float32)
    for copy in copies:
        copy.wait()


def power_of_two(n, low):
    result = jnp.full(n.shape, 2.0**low, jnp.float32)
    for bit in range(7):
        factor = jnp.where(((n - low) >> bit) & 1 == 1, jnp.float32(2.0 ** (2**bit)), jnp.float32(1.0))
        result = result * factor
    return result


def encode(total):
    groups = total.reshape(N_GROUP, 16, BS)
    largest = jnp.max(jnp.abs(groups), axis=1)
    exponent = jnp.floor(jnp.log2(jnp.maximum(largest, 2.0**-100))).astype(jnp.int32) + 1
    scaled = groups * power_of_two(15 - exponent, -13)[:, None, :]
    rounded = jnp.clip(jnp.floor(scaled + 0.5), -32767.0, 32767.0).astype(jnp.int32)
    return rounded.reshape(SLAB, BS).astype(jnp.int16), exponent.astype(jnp.int16)


def decode(parts_ref, q):
    groups = parts_ref[q, :SLAB, :].astype(jnp.int32).astype(jnp.float32).reshape(N_GROUP, 16, BS)
    scale = power_of_two(parts_ref[q, SLAB:, :].astype(jnp.int32) - 15, -115)
    return (groups * scale[:, None, :]).reshape(SLAB, BS)


def multiply(s_ref, sk_ref, mk_ref, out_ref):
    for z in range(N_Z):
        sk_ref[:, z * BS:(z + 1) * BS] = s_ref[z]
    total = jnp.dot(sk_ref[...], mk_ref[...], preferred_element_type=jnp.float32)
    for q in range(N_YH):
        out_ref[q, :SLAB, :], out_ref[q, SLAB:, :] = encode(total[:, q * BS:(q + 1) * BS])


def first_product(s_ref, mine_ref, other_ref, out_ref, mk_ref, sk_ref):
    my_core, yh = lax.axis_index("core"), lax.axis_index("yh")
    for z in range(N_Z):
        r = lax.div(4 * z + yh, 3)
        slot = lax.div(r, 2) * N_YH
        here = lax.rem(r, 2) == my_core

        @pl.when(here)
        def _():
            for q in range(N_YH):
                mk_ref[z * BS:(z + 1) * BS, q * BS:(q + 1) * BS] = mine_ref[slot + q]

        @pl.when(jnp.logical_not(here))
        def _():
            for q in range(N_YH):
                mk_ref[z * BS:(z + 1) * BS, q * BS:(q + 1) * BS] = other_ref[slot + q]

    multiply(s_ref, sk_ref, mk_ref, out_ref)


def second_product(s_ref, mk_ref, out_ref, sk_ref):
    multiply(s_ref, sk_ref, mk_ref, out_ref)


def add_parts(parts_ref):
    return (decode(parts_ref, 0) + decode(parts_ref, 1)) + (decode(parts_ref, 2) + decode(parts_ref, 3))


def finish_square(mask_ref, parts_ref, out_ref):
    total = add_parts(parts_ref)
    for t in range(2):
        rows = slice(t * BS, (t + 1) * BS)
        out_ref[rows, :] = (total[rows] * FACTOR * mask_ref[t * 8:t * 8 + 1, :]).astype(jnp.bfloat16)


def finish_sign(mask_ref, slab_ref, parts_ref, out_ref):
    total = add_parts(parts_ref)
    for t in range(2):
        rows = slice(t * BS, (t + 1) * BS)
        step = 1.5 * slab_ref[rows, :].astype(jnp.float32) - 0.5 * FACTOR * total[rows]
        out_ref[rows, :] = (step * mask_ref[t * 8:t * 8 + 1, :]).astype(jnp.bfloat16)


def shape(*dims, dtype=jnp.bfloat16):
    return jax.ShapeDtypeStruct(dims, dtype)


def kernel(body, n_in, out_shape, scratch=(), flops=0, moved=1 << 20):
    return pl.pallas_call(
        body,
        out_shape=out_shape,
        in_specs=vmem(n_in),
        out_specs=jax.tree.map(lambda _: pl.BlockSpec(memory_space=pltpu.VMEM), out_shape),
        scratch_shapes=list(scratch),
        compiler_params=pltpu.CompilerParams(vmem_limit_bytes=LIMIT),
        cost_estimate=pl.CostEstimate(flops=flops, bytes_accessed=moved, transcendentals=0),
    )


def local(values, occupancy):
    group = N_YL * N_X * N_YH
    anywhere, in_vmem = pl.BlockSpec(memory_space=pl.ANY), pl.BlockSpec(memory_space=pltpu.VMEM)
    slab, mask, send = pl.pallas_call(
        prepare,
        out_shape=(shape(SLAB, BS), shape(16, BS, dtype=jnp.float32), shape(group, BS, BS)),
        in_specs=[anywhere, anywhere],
        out_specs=(in_vmem, in_vmem, anywhere),
        scratch_shapes=[
            pltpu.SMEM((3,), jnp.int32),
            pltpu.VMEM((3 * BS, BS), jnp.bfloat16),
            pltpu.VMEM((N_YH, BS, BS), jnp.bfloat16),
            pltpu.SemaphoreType.DMA((2,)),
            pltpu.SemaphoreType.DMA((N_YL * N_X,)),
        ],
        compiler_params=pltpu.CompilerParams(vmem_limit_bytes=60 * 1024 * 1024),
    )(occupancy.reshape(3), values)
    mine = lax.all_to_all(send, ("yl", "x", "yh"), 0, 0, tiled=True)
    gathered = lax.all_gather(slab, "z", axis=0, tiled=False)
    mine, gathered = lax.optimization_barrier((mine, gathered))
    other = lax.ppermute(mine, "core", [(0, 1), (1, 0)])
    cost = dict(flops=2 * SLAB * 12 * BS * 4 * BS, moved=4 << 20)
    sk = pltpu.VMEM((SLAB, N_Z * BS), jnp.bfloat16)
    parts_shape = shape(N_YH, SLAB + N_GROUP, BS, dtype=jnp.int16)
    parts, mk = kernel(
        first_product, 3, (parts_shape, shape(N_Z * BS, N_YH * BS)), (sk,), **cost
    )(gathered, mine, other)
    parts = lax.all_to_all(parts, "yh", 0, 0, tiled=True)
    square_slab = kernel(finish_square, 2, shape(SLAB, BS))(mask, parts)
    gathered = lax.all_gather(square_slab, "z", axis=0, tiled=False)
    parts = kernel(second_product, 2, parts_shape, (sk,), **cost)(gathered, mk)
    parts = lax.all_to_all(parts, "yh", 0, 0, tiled=True)
    sign_step = kernel(finish_sign, 3, shape(SLAB, BS))(mask, slab, parts)
    return (square_slab, sign_step)


def solution(mesh):
    fine = Mesh(
        mesh.devices.reshape(N_YL, N_X, N_CORE, N_Z, N_YH), ("yl", "x", "core", "z", "yh")
    )
    spec = P(("yl", "x", "core"), ("z", "yh"))
    return jax.shard_map(local, mesh=fine, in_specs=(spec, spec), out_specs=(spec, spec), check_vma=False)
```

```python
import math

import jax
import jax.numpy as jnp
from jax import lax
from jax.experimental import pallas as pl
from jax.experimental.pallas import tpu as pltpu
from jax.sharding import Mesh
from jax.sharding import PartitionSpec as P

BS = 128
SLAB = 256
ORDER = 6144
FACTOR = 1.0 / math.sqrt(ORDER)
N_YL, N_X, N_CORE, N_Z, N_YH = 2, 4, 2, 12, 4
N_GROUP = SLAB // 16
LIMIT = 24 * 1024 * 1024


def vmem(n):
    return [pl.BlockSpec(memory_space=pltpu.VMEM)] * n


def row_index():
    return (lax.axis_index("yl") * N_X + lax.axis_index("x")) * N_CORE + lax.axis_index("core")


def prepare(occ_hbm, values_hbm, slab_ref, mask_ref, send_hbm, occ_ref, values_ref, blocks_ref, in_sem, out_sem):
    copies = [
        pltpu.make_async_copy(occ_hbm, occ_ref, in_sem.at[0]),
        pltpu.make_async_copy(values_hbm, values_ref, in_sem.at[1]),
    ]
    for copy in copies:
        copy.start()
    for copy in copies:
        copy.wait()
    first = 3 * row_index()
    for q in range(N_YH):
        t = lax.rem(q + 4 * 48 - first, 4)
        held = jnp.minimum(t, 2)
        keep = jnp.where(t < 3, occ_ref[held], 0).astype(jnp.float32).astype(jnp.bfloat16)
        blocks_ref[q] = values_ref[pl.ds(pl.multiple_of(held * BS, BS), BS), :] * keep
    copies = [
        pltpu.make_async_copy(blocks_ref, send_hbm.at[pl.ds(j * N_YH, N_YH)], out_sem.at[j])
        for j in range(N_YL * N_X)
    ]
    for copy in copies:
        copy.start()
    for t in range(2):
        rows = pl.ds(t * BS, BS)
        keep = occ_ref[t].astype(jnp.float32)
        slab_ref[rows, :] = values_ref[rows, :] * keep.astype(jnp.bfloat16)
        mask_ref[t * 8:(t + 1) * 8, :] = jnp.full((8, BS), keep, jnp.float32)
    for copy in copies:
        copy.wait()


def power_of_two(n, low):
    result = jnp.full(n.shape, 2.0**low, jnp.float32)
    for bit in range(7):
        factor = jnp.where(((n - low) >> bit) & 1 == 1, jnp.float32(2.0 ** (2**bit)), jnp.float32(1.0))
        result = result * factor
    return result


def encode(total):
    groups = total.reshape(N_GROUP, 16, BS)
    largest = jnp.max(jnp.abs(groups), axis=1)
    exponent = jnp.floor(jnp.log2(jnp.maximum(largest, 2.0**-100))).astype(jnp.int32) + 1
    scaled = groups * power_of_two(15 - exponent, -13)[:, None, :]
    rounded = jnp.clip(jnp.floor(scaled + 0.5), -32767.0, 32767.0).astype(jnp.int32)
    return rounded.reshape(SLAB, BS).astype(jnp.int16), exponent.astype(jnp.int16)


def decode(parts_ref, q):
    groups = parts_ref[q, :SLAB, :].astype(jnp.int32).astype(jnp.float32).reshape(N_GROUP, 16, BS)
    scale = power_of_two(parts_ref[q, SLAB:, :].astype(jnp.int32) - 15, -115)
    return (groups * scale[:, None, :]).reshape(SLAB, BS)


def multiply(s_ref, mk_ref, out_ref):
    total = jnp.dot(s_ref[...], mk_ref[...], preferred_element_type=jnp.float32)
    for q in range(N_YH):
        out_ref[q, :SLAB, :], out_ref[q, SLAB:, :] = encode(total[:, q * BS:(q + 1) * BS])


def first_product(s_ref, mine_ref, other_ref, out_ref, mk_ref):
    my_core, yh = lax.axis_index("core"), lax.axis_index("yh")
    for z in range(N_Z):
        r = lax.div(4 * z + yh, 3)
        slot = lax.div(r, 2) * N_YH
        here = lax.rem(r, 2) == my_core

        @pl.when(here)
        def _():
            for q in range(N_YH):
                mk_ref[z * BS:(z + 1) * BS, q * BS:(q + 1) * BS] = mine_ref[slot + q]

        @pl.when(jnp.logical_not(here))
        def _():
            for q in range(N_YH):
                mk_ref[z * BS:(z + 1) * BS, q * BS:(q + 1) * BS] = other_ref[slot + q]

    multiply(s_ref, mk_ref, out_ref)


def second_product(s_ref, mk_ref, out_ref):
    multiply(s_ref, mk_ref, out_ref)


def add_parts(parts_ref):
    return (decode(parts_ref, 0) + decode(parts_ref, 1)) + (decode(parts_ref, 2) + decode(parts_ref, 3))


def finish_square(mask_ref, parts_ref, out_ref):
    total = add_parts(parts_ref)
    for t in range(2):
        rows = slice(t * BS, (t + 1) * BS)
        out_ref[rows, :] = (total[rows] * FACTOR * mask_ref[t * 8:t * 8 + 1, :]).astype(jnp.bfloat16)


def finish_sign(mask_ref, slab_ref, parts_ref, out_ref):
    total = add_parts(parts_ref)
    for t in range(2):
        rows = slice(t * BS, (t + 1) * BS)
        step = 1.5 * slab_ref[rows, :].astype(jnp.float32) - 0.5 * FACTOR * total[rows]
        out_ref[rows, :] = (step * mask_ref[t * 8:t * 8 + 1, :]).astype(jnp.bfloat16)


def shape(*dims, dtype=jnp.bfloat16):
    return jax.ShapeDtypeStruct(dims, dtype)


def kernel(body, n_in, out_shape, flops=0, moved=1 << 20):
    return pl.pallas_call(
        body,
        out_shape=out_shape,
        in_specs=vmem(n_in),
        out_specs=jax.tree.map(lambda _: pl.BlockSpec(memory_space=pltpu.VMEM), out_shape),
        compiler_params=pltpu.CompilerParams(vmem_limit_bytes=LIMIT),
        cost_estimate=pl.CostEstimate(flops=flops, bytes_accessed=moved, transcendentals=0),
    )


def local(values, occupancy):
    group = N_YL * N_X * N_YH
    anywhere, in_vmem = pl.BlockSpec(memory_space=pl.ANY), pl.BlockSpec(memory_space=pltpu.VMEM)
    slab, mask, send = pl.pallas_call(
        prepare,
        out_shape=(shape(SLAB, BS), shape(16, BS, dtype=jnp.float32), shape(group, BS, BS)),
        in_specs=[anywhere, anywhere],
        out_specs=(in_vmem, in_vmem, anywhere),
        scratch_shapes=[
            pltpu.SMEM((3,), jnp.int32),
            pltpu.VMEM((3 * BS, BS), jnp.bfloat16),
            pltpu.VMEM((N_YH, BS, BS), jnp.bfloat16),
            pltpu.SemaphoreType.DMA((2,)),
            pltpu.SemaphoreType.DMA((N_YL * N_X,)),
        ],
        compiler_params=pltpu.CompilerParams(vmem_limit_bytes=60 * 1024 * 1024),
    )(occupancy.reshape(3), values)
    mine = lax.all_to_all(send, ("yl", "x", "yh"), 0, 0, tiled=True)
    gathered = lax.all_gather(slab, "z", axis=1, tiled=True)
    mine, gathered = lax.optimization_barrier((mine, gathered))
    other = lax.ppermute(mine, "core", [(0, 1), (1, 0)])
    cost = dict(flops=2 * SLAB * 12 * BS * 4 * BS, moved=4 << 20)
    parts_shape = shape(N_YH, SLAB + N_GROUP, BS, dtype=jnp.int16)
    mk_shape = shape(N_Z * BS, N_YH * BS)
    parts, mk = kernel(first_product, 3, (parts_shape, mk_shape), **cost)(gathered, mine, other)
    parts = lax.all_to_all(parts, "yh", 0, 0, tiled=True)
    square_slab = kernel(finish_square, 2, shape(SLAB, BS))(mask, parts)
    gathered = lax.all_gather(square_slab, "z", axis=1, tiled=True)
    parts = kernel(second_product, 2, parts_shape, **cost)(gathered, mk)
    parts = lax.all_to_all(parts, "yh", 0, 0, tiled=True)
    sign_step = kernel(finish_sign, 3, shape(SLAB, BS))(mask, slab, parts)
    return (square_slab, sign_step)


def solution(mesh):
    fine = Mesh(
        mesh.devices.reshape(N_YL, N_X, N_CORE, N_Z, N_YH), ("yl", "x", "core", "z", "yh")
    )
    spec = P(("yl", "x", "core"), ("z", "yh"))
    return jax.shard_map(local, mesh=fine, in_specs=(spec, spec), out_specs=(spec, spec), check_vma=False)
```

```python
import math

import jax
import jax.numpy as jnp
from jax import lax
from jax.experimental import pallas as pl
from jax.experimental.pallas import tpu as pltpu
from jax.sharding import Mesh
from jax.sharding import PartitionSpec as P

BS = 128
SLAB = 256
ORDER = 6144
FACTOR = 1.0 / math.sqrt(ORDER)
N_YL, N_X, N_CORE, N_Z, N_YH = 2, 4, 2, 12, 4
N_GROUP = SLAB // 16
LIMIT = 24 * 1024 * 1024


def vmem(n):
    return [pl.BlockSpec(memory_space=pltpu.VMEM)] * n


def row_index():
    return (lax.axis_index("yl") * N_X + lax.axis_index("x")) * N_CORE + lax.axis_index("core")


def prepare(
    occ_hbm, values_hbm, slab_hbm, mask_hbm, send_hbm,
    occ_ref, values_ref, slab_ref, mask_ref, blocks_ref, in_sem, out_sem, send_sem,
):
    read = [
        pltpu.make_async_copy(occ_hbm, occ_ref, in_sem.at[0]),
        pltpu.make_async_copy(values_hbm, values_ref, in_sem.at[1]),
    ]
    for copy in read:
        copy.start()
    for copy in read:
        copy.wait()
    written = []
    first = 3 * row_index()
    for q in range(N_YH):
        t = lax.rem(q + 4 * 48 - first, 4)
        held = jnp.minimum(t, 2)
        keep = jnp.where(t < 3, occ_ref[held], 0).astype(jnp.float32).astype(jnp.bfloat16)
        blocks_ref[q] = values_ref[pl.ds(pl.multiple_of(held * BS, BS), BS), :] * keep
    for j in range(N_YL * N_X):
        copy = pltpu.make_async_copy(blocks_ref, send_hbm.at[pl.ds(j * N_YH, N_YH)], send_sem.at[j])
        copy.start()
        written.append(copy)
    for t in range(2):
        rows = pl.ds(t * BS, BS)
        keep = occ_ref[t].astype(jnp.float32)
        slab_ref[rows, :] = values_ref[rows, :] * keep.astype(jnp.bfloat16)
        mask_ref[t * 8:(t + 1) * 8, :] = jnp.full((8, BS), keep, jnp.float32)
    for i, (source, target) in enumerate(((slab_ref, slab_hbm), (mask_ref, mask_hbm))):
        copy = pltpu.make_async_copy(source, target, out_sem.at[i])
        copy.start()
        written.append(copy)
    for copy in written:
        copy.wait()


def power_of_two(n, low):
    result = jnp.full(n.shape, 2.0**low, jnp.float32)
    for bit in range(7):
        factor = jnp.where(((n - low) >> bit) & 1 == 1, jnp.float32(2.0 ** (2**bit)), jnp.float32(1.0))
        result = result * factor
    return result


def encode(total):
    groups = total.reshape(N_GROUP, 16, BS)
    largest = jnp.max(jnp.abs(groups), axis=1)
    exponent = jnp.floor(jnp.log2(jnp.maximum(largest, 2.0**-100))).astype(jnp.int32) + 1
    scaled = groups * power_of_two(15 - exponent, -13)[:, None, :]
    rounded = jnp.clip(jnp.floor(scaled + 0.5), -32767.0, 32767.0).astype(jnp.int32)
    return rounded.reshape(SLAB, BS).astype(jnp.int16), exponent.astype(jnp.int16)


def decode(parts_ref, q):
    groups = parts_ref[q, :SLAB, :].astype(jnp.int32).astype(jnp.float32).reshape(N_GROUP, 16, BS)
    scale = power_of_two(parts_ref[q, SLAB:, :].astype(jnp.int32) - 15, -115)
    return (groups * scale[:, None, :]).reshape(SLAB, BS)


def multiply(s_ref, mk_ref, out_ref):
    total = jnp.dot(s_ref[...], mk_ref[...], preferred_element_type=jnp.float32)
    for q in range(N_YH):
        out_ref[q, :SLAB, :], out_ref[q, SLAB:, :] = encode(total[:, q * BS:(q + 1) * BS])


def first_product(s_ref, mine_ref, other_ref, out_ref, mk_ref):
    my_core, yh = lax.axis_index("core"), lax.axis_index("yh")
    for z in range(N_Z):
        r = lax.div(4 * z + yh, 3)
        slot = lax.div(r, 2) * N_YH
        here = lax.rem(r, 2) == my_core

        @pl.when(here)
        def _():
            for q in range(N_YH):
                mk_ref[z * BS:(z + 1) * BS, q * BS:(q + 1) * BS] = mine_ref[slot + q]

        @pl.when(jnp.logical_not(here))
        def _():
            for q in range(N_YH):
                mk_ref[z * BS:(z + 1) * BS, q * BS:(q + 1) * BS] = other_ref[slot + q]

    multiply(s_ref, mk_ref, out_ref)


def second_product(s_ref, mk_ref, out_ref):
    multiply(s_ref, mk_ref, out_ref)


def add_parts(parts_ref):
    return (decode(parts_ref, 0) + decode(parts_ref, 1)) + (decode(parts_ref, 2) + decode(parts_ref, 3))


def finish_square(mask_ref, parts_ref, out_ref):
    total = add_parts(parts_ref)
    for t in range(2):
        rows = slice(t * BS, (t + 1) * BS)
        out_ref[rows, :] = (total[rows] * FACTOR * mask_ref[t * 8:t * 8 + 1, :]).astype(jnp.bfloat16)


def finish_sign(mask_ref, slab_ref, parts_ref, out_ref):
    total = add_parts(parts_ref)
    for t in range(2):
        rows = slice(t * BS, (t + 1) * BS)
        step = 1.5 * slab_ref[rows, :].astype(jnp.float32) - 0.5 * FACTOR * total[rows]
        out_ref[rows, :] = (step * mask_ref[t * 8:t * 8 + 1, :]).astype(jnp.bfloat16)


def shape(*dims, dtype=jnp.bfloat16):
    return jax.ShapeDtypeStruct(dims, dtype)


def kernel(body, n_in, out_shape, flops=0, moved=1 << 20):
    return pl.pallas_call(
        body,
        out_shape=out_shape,
        in_specs=vmem(n_in),
        out_specs=jax.tree.map(lambda _: pl.BlockSpec(memory_space=pltpu.VMEM), out_shape),
        compiler_params=pltpu.CompilerParams(vmem_limit_bytes=LIMIT),
        cost_estimate=pl.CostEstimate(flops=flops, bytes_accessed=moved, transcendentals=0),
    )


def local(values, occupancy):
    group = N_YL * N_X * N_YH
    anywhere = pl.BlockSpec(memory_space=pl.ANY)
    slab, mask, send = pl.pallas_call(
        prepare,
        out_shape=(shape(SLAB, BS), shape(16, BS, dtype=jnp.float32), shape(group, BS, BS)),
        in_specs=[anywhere, anywhere],
        out_specs=(anywhere, anywhere, anywhere),
        scratch_shapes=[
            pltpu.SMEM((3,), jnp.int32),
            pltpu.VMEM((3 * BS, BS), jnp.bfloat16),
            pltpu.VMEM((SLAB, BS), jnp.bfloat16),
            pltpu.VMEM((16, BS), jnp.float32),
            pltpu.VMEM((N_YH, BS, BS), jnp.bfloat16),
            pltpu.SemaphoreType.DMA((2,)),
            pltpu.SemaphoreType.DMA((2,)),
            pltpu.SemaphoreType.DMA((N_YL * N_X,)),
        ],
        compiler_params=pltpu.CompilerParams(vmem_limit_bytes=60 * 1024 * 1024),
    )(occupancy.reshape(3), values)
    mine = lax.all_to_all(send, ("yl", "x", "yh"), 0, 0, tiled=True)
    gathered = lax.all_gather(slab, "z", axis=1, tiled=True)
    mine, gathered = lax.optimization_barrier((mine, gathered))
    other = lax.ppermute(mine, "core", [(0, 1), (1, 0)])
    cost = dict(flops=2 * SLAB * 12 * BS * 4 * BS, moved=4 << 20)
    parts_shape = shape(N_YH, SLAB + N_GROUP, BS, dtype=jnp.int16)
    mk_shape = shape(N_Z * BS, N_YH * BS)
    parts, mk = kernel(first_product, 3, (parts_shape, mk_shape), **cost)(gathered, mine, other)
    parts = lax.all_to_all(parts, "yh", 0, 0, tiled=True)
    square_slab = kernel(finish_square, 2, shape(SLAB, BS))(mask, parts)
    gathered = lax.all_gather(square_slab, "z", axis=1, tiled=True)
    parts = kernel(second_product, 2, parts_shape, **cost)(gathered, mk)
    parts = lax.all_to_all(parts, "yh", 0, 0, tiled=True)
    sign_step = kernel(finish_sign, 3, shape(SLAB, BS))(mask, slab, parts)
    return (square_slab, sign_step)


def solution(mesh):
    fine = Mesh(
        mesh.devices.reshape(N_YL, N_X, N_CORE, N_Z, N_YH), ("yl", "x", "core", "z", "yh")
    )
    spec = P(("yl", "x", "core"), ("z", "yh"))
    return jax.shard_map(local, mesh=fine, in_specs=(spec, spec), out_specs=(spec, spec), check_vma=False)
```

```python
import math

import jax
import jax.numpy as jnp
from jax import lax
from jax.experimental import pallas as pl
from jax.experimental.pallas import tpu as pltpu
from jax.sharding import Mesh
from jax.sharding import PartitionSpec as P

BS = 128
SLAB = 256
ORDER = 6144
FACTOR = 1.0 / math.sqrt(ORDER)
N_YL, N_X, N_CORE, N_Z, N_YH = 2, 4, 2, 12, 4
N_GROUP = SLAB // 16
LIMIT = 24 * 1024 * 1024


def vmem(n):
    return [pl.BlockSpec(memory_space=pltpu.VMEM)] * n


def row_index():
    return (lax.axis_index("yl") * N_X + lax.axis_index("x")) * N_CORE + lax.axis_index("core")


def prepare(
    occ_hbm, values_hbm, slab_hbm, mask_hbm, send_hbm,
    occ_ref, values_ref, slab_ref, mask_ref, blocks_ref, in_sem, out_sem, send_sem,
):
    read = [
        pltpu.make_async_copy(occ_hbm, occ_ref, in_sem.at[0]),
        pltpu.make_async_copy(values_hbm, values_ref, in_sem.at[1]),
    ]
    for copy in read:
        copy.start()
    for copy in read:
        copy.wait()
    written = []
    first = 3 * row_index()
    for q in range(N_YH):
        t = lax.rem(q + 4 * 48 - first, 4)
        held = jnp.minimum(t, 2)
        keep = jnp.where(t < 3, occ_ref[held], 0).astype(jnp.float32).astype(jnp.bfloat16)
        blocks_ref[q] = values_ref[pl.ds(pl.multiple_of(held * BS, BS), BS), :] * keep
    for j in range(N_YL * N_X):
        copy = pltpu.make_async_copy(blocks_ref, send_hbm.at[pl.ds(j * N_YH, N_YH)], send_sem.at[j])
        copy.start()
        written.append(copy)
    for t in range(2):
        rows = pl.ds(t * BS, BS)
        keep = occ_ref[t].astype(jnp.float32)
        slab_ref[rows, :] = values_ref[rows, :] * keep.astype(jnp.bfloat16)
        mask_ref[t * 8:(t + 1) * 8, :] = jnp.full((8, BS), keep, jnp.float32)
    for i, (source, target) in enumerate(((slab_ref, slab_hbm), (mask_ref, mask_hbm))):
        copy = pltpu.make_async_copy(source, target, out_sem.at[i])
        copy.start()
        written.append(copy)
    for copy in written:
        copy.wait()


def power_of_two(n, low):
    result = jnp.full(n.shape, 2.0**low, jnp.float32)
    for bit in range(7):
        factor = jnp.where(((n - low) >> bit) & 1 == 1, jnp.float32(2.0 ** (2**bit)), jnp.float32(1.0))
        result = result * factor
    return result


def encode(total):
    groups = total.reshape(N_GROUP, 16, BS)
    largest = jnp.max(jnp.abs(groups), axis=1)
    exponent = jnp.floor(jnp.log2(jnp.maximum(largest, 2.0**-100))).astype(jnp.int32) + 1
    scaled = groups * power_of_two(15 - exponent, -13)[:, None, :]
    rounded = jnp.clip(jnp.floor(scaled + 0.5), -32767.0, 32767.0).astype(jnp.int32)
    return rounded.reshape(SLAB, BS).astype(jnp.int16), exponent.astype(jnp.int16)


def decode(parts_ref, q):
    groups = parts_ref[q, :SLAB, :].astype(jnp.int32).astype(jnp.float32).reshape(N_GROUP, 16, BS)
    scale = power_of_two(parts_ref[q, SLAB:, :].astype(jnp.int32) - 15, -115)
    return (groups * scale[:, None, :]).reshape(SLAB, BS)


def multiply(s_ref, mk_ref, out_ref):
    total = jnp.dot(s_ref[...], mk_ref[...], preferred_element_type=jnp.float32)
    for q in range(N_YH):
        out_ref[q, :SLAB, :], out_ref[q, SLAB:, :] = encode(total[:, q * BS:(q + 1) * BS])


def first_product(s_ref, mine_ref, other_ref, out_ref, mk_ref):
    my_core, yh = lax.axis_index("core"), lax.axis_index("yh")
    for z in range(N_Z):
        r = lax.div(4 * z + yh, 3)
        slot = lax.div(r, 2) * N_YH
        here = lax.rem(r, 2) == my_core

        @pl.when(here)
        def _():
            for q in range(N_YH):
                mk_ref[z * BS:(z + 1) * BS, q * BS:(q + 1) * BS] = mine_ref[slot + q]

        @pl.when(jnp.logical_not(here))
        def _():
            for q in range(N_YH):
                mk_ref[z * BS:(z + 1) * BS, q * BS:(q + 1) * BS] = other_ref[slot + q]

    multiply(s_ref, mk_ref, out_ref)


def second_product(s_ref, mk_ref, square_ref, out_ref, square_hbm, sem):
    copy = pltpu.make_async_copy(square_ref, square_hbm, sem)
    copy.start()
    multiply(s_ref, mk_ref, out_ref)
    copy.wait()


def add_parts(parts_ref):
    return (decode(parts_ref, 0) + decode(parts_ref, 1)) + (decode(parts_ref, 2) + decode(parts_ref, 3))


def finish_square(mask_ref, parts_ref, out_ref):
    total = add_parts(parts_ref)
    for t in range(2):
        rows = slice(t * BS, (t + 1) * BS)
        out_ref[rows, :] = (total[rows] * FACTOR * mask_ref[t * 8:t * 8 + 1, :]).astype(jnp.bfloat16)


def finish_sign(mask_ref, slab_ref, parts_ref, out_ref):
    total = add_parts(parts_ref)
    for t in range(2):
        rows = slice(t * BS, (t + 1) * BS)
        step = 1.5 * slab_ref[rows, :].astype(jnp.float32) - 0.5 * FACTOR * total[rows]
        out_ref[rows, :] = (step * mask_ref[t * 8:t * 8 + 1, :]).astype(jnp.bfloat16)


def shape(*dims, dtype=jnp.bfloat16):
    return jax.ShapeDtypeStruct(dims, dtype)


def kernel(body, n_in, out_shape, flops=0, moved=1 << 20):
    return pl.pallas_call(
        body,
        out_shape=out_shape,
        in_specs=vmem(n_in),
        out_specs=jax.tree.map(lambda _: pl.BlockSpec(memory_space=pltpu.VMEM), out_shape),
        compiler_params=pltpu.CompilerParams(vmem_limit_bytes=LIMIT),
        cost_estimate=pl.CostEstimate(flops=flops, bytes_accessed=moved, transcendentals=0),
    )


def local(values, occupancy):
    group = N_YL * N_X * N_YH
    anywhere = pl.BlockSpec(memory_space=pl.ANY)
    slab, mask, send = pl.pallas_call(
        prepare,
        out_shape=(shape(SLAB, BS), shape(16, BS, dtype=jnp.float32), shape(group, BS, BS)),
        in_specs=[anywhere, anywhere],
        out_specs=(anywhere, anywhere, anywhere),
        scratch_shapes=[
            pltpu.SMEM((3,), jnp.int32),
            pltpu.VMEM((3 * BS, BS), jnp.bfloat16),
            pltpu.VMEM((SLAB, BS), jnp.bfloat16),
            pltpu.VMEM((16, BS), jnp.float32),
            pltpu.VMEM((N_YH, BS, BS), jnp.bfloat16),
            pltpu.SemaphoreType.DMA((2,)),
            pltpu.SemaphoreType.DMA((2,)),
            pltpu.SemaphoreType.DMA((N_YL * N_X,)),
        ],
        compiler_params=pltpu.CompilerParams(vmem_limit_bytes=60 * 1024 * 1024),
    )(occupancy.reshape(3), values)
    mine = lax.all_to_all(send, ("yl", "x", "yh"), 0, 0, tiled=True)
    gathered = lax.all_gather(slab, "z", axis=1, tiled=True)
    mine, gathered = lax.optimization_barrier((mine, gathered))
    other = lax.ppermute(mine, "core", [(0, 1), (1, 0)])
    cost = dict(flops=2 * SLAB * 12 * BS * 4 * BS, moved=4 << 20)
    parts_shape = shape(N_YH, SLAB + N_GROUP, BS, dtype=jnp.int16)
    mk_shape = shape(N_Z * BS, N_YH * BS)
    parts, mk = kernel(first_product, 3, (parts_shape, mk_shape), **cost)(gathered, mine, other)
    parts = lax.all_to_all(parts, "yh", 0, 0, tiled=True)
    square = kernel(finish_square, 2, shape(SLAB, BS))(mask, parts)
    gathered = lax.all_gather(square, "z", axis=1, tiled=True)
    parts, square_slab = pl.pallas_call(
        second_product,
        out_shape=(parts_shape, shape(SLAB, BS)),
        in_specs=vmem(3),
        out_specs=(pl.BlockSpec(memory_space=pltpu.VMEM), anywhere),
        scratch_shapes=[pltpu.SemaphoreType.DMA],
        compiler_params=pltpu.CompilerParams(vmem_limit_bytes=LIMIT),
        cost_estimate=pl.CostEstimate(flops=cost["flops"], bytes_accessed=cost["moved"], transcendentals=0),
    )(gathered, mk, square)
    parts = lax.all_to_all(parts, "yh", 0, 0, tiled=True)
    sign_step = kernel(finish_sign, 3, shape(SLAB, BS))(mask, slab, parts)
    return (square_slab, sign_step)


def solution(mesh):
    fine = Mesh(
        mesh.devices.reshape(N_YL, N_X, N_CORE, N_Z, N_YH), ("yl", "x", "core", "z", "yh")
    )
    spec = P(("yl", "x", "core"), ("z", "yh"))
    return jax.shard_map(local, mesh=fine, in_specs=(spec, spec), out_specs=(spec, spec), check_vma=False)
```

```python
import math

import jax
import jax.numpy as jnp
from jax import lax
from jax.experimental import pallas as pl
from jax.experimental.pallas import tpu as pltpu
from jax.sharding import Mesh
from jax.sharding import PartitionSpec as P

BS = 128
SLAB = 256
ORDER = 6144
FACTOR = 1.0 / math.sqrt(ORDER)
N_YL, N_X, N_CORE, N_Z, N_YH = 2, 4, 2, 12, 4
N_GROUP = SLAB // 16
PLACES = [2, 3, 0, 1]
LIMIT = 24 * 1024 * 1024


def vmem(n):
    return [pl.BlockSpec(memory_space=pltpu.VMEM)] * n


def row_index():
    return (lax.axis_index("yl") * N_X + lax.axis_index("x")) * N_CORE + lax.axis_index("core")


def prepare(
    occ_hbm, values_hbm, slab_hbm, mask_hbm, send_hbm,
    occ_ref, values_ref, slab_ref, mask_ref, blocks_ref, in_sem, out_sem, send_sem,
):
    read = [
        pltpu.make_async_copy(occ_hbm, occ_ref, in_sem.at[0]),
        pltpu.make_async_copy(values_hbm, values_ref, in_sem.at[1]),
    ]
    for copy in read:
        copy.start()
    for copy in read:
        copy.wait()
    written = []
    first = 3 * row_index()
    for q in range(N_YH):
        t = lax.rem(q + 4 * 48 - first, 4)
        held = jnp.minimum(t, 2)
        keep = jnp.where(t < 3, occ_ref[held], 0).astype(jnp.float32).astype(jnp.bfloat16)
        blocks_ref[q] = values_ref[pl.ds(pl.multiple_of(held * BS, BS), BS), :] * keep
    for j in range(N_YL * N_X):
        copy = pltpu.make_async_copy(blocks_ref, send_hbm.at[pl.ds(j * N_YH, N_YH)], send_sem.at[j])
        copy.start()
        written.append(copy)
    for t in range(2):
        rows = pl.ds(t * BS, BS)
        keep = occ_ref[t].astype(jnp.float32)
        slab_ref[rows, :] = values_ref[rows, :] * keep.astype(jnp.bfloat16)
        mask_ref[t * 8:(t + 1) * 8, :] = jnp.full((8, BS), keep, jnp.float32)
    for i, (source, target) in enumerate(((slab_ref, slab_hbm), (mask_ref, mask_hbm))):
        copy = pltpu.make_async_copy(source, target, out_sem.at[i])
        copy.start()
        written.append(copy)
    for copy in written:
        copy.wait()


def power_of_two(n, low):
    result = jnp.full(n.shape, 2.0**low, jnp.float32)
    for bit in range(7):
        factor = jnp.where(((n - low) >> bit) & 1 == 1, jnp.float32(2.0 ** (2**bit)), jnp.float32(1.0))
        result = result * factor
    return result


def encode(total):
    groups = total.reshape(N_GROUP, 16, BS)
    largest = jnp.max(jnp.abs(groups), axis=1)
    exponent = jnp.floor(jnp.log2(jnp.maximum(largest, 2.0**-100))).astype(jnp.int32) + 1
    scaled = groups * power_of_two(15 - exponent, -13)[:, None, :]
    rounded = jnp.clip(jnp.floor(scaled + 0.5), -32767.0, 32767.0).astype(jnp.int32)
    return rounded.reshape(SLAB, BS).astype(jnp.int16), exponent.astype(jnp.int16)


def decode(parts_ref, q):
    groups = parts_ref[q, :SLAB, :].astype(jnp.int32).astype(jnp.float32).reshape(N_GROUP, 16, BS)
    scale = power_of_two(parts_ref[q, SLAB:, :].astype(jnp.int32) - 15, -115)
    return (groups * scale[:, None, :]).reshape(SLAB, BS)


def multiply(s_ref, mk_ref, out_ref):
    total = jnp.dot(s_ref[...], mk_ref[...], preferred_element_type=jnp.float32)
    for q in range(N_YH):
        at = PLACES.index(q)
        out_ref[at, :SLAB, :], out_ref[at, SLAB:, :] = encode(total[:, q * BS:(q + 1) * BS])


def first_product(s_ref, mine_ref, other_ref, out_ref, mk_ref):
    my_core, yh = lax.axis_index("core"), lax.axis_index("yh")
    for z in range(N_Z):
        r = lax.div(4 * z + yh, 3)
        slot = lax.div(r, 2) * N_YH
        here = lax.rem(r, 2) == my_core

        @pl.when(here)
        def _():
            for q in range(N_YH):
                mk_ref[z * BS:(z + 1) * BS, q * BS:(q + 1) * BS] = mine_ref[slot + q]

        @pl.when(jnp.logical_not(here))
        def _():
            for q in range(N_YH):
                mk_ref[z * BS:(z + 1) * BS, q * BS:(q + 1) * BS] = other_ref[slot + q]

    multiply(s_ref, mk_ref, out_ref)


def second_product(s_ref, mk_ref, square_ref, out_ref, square_hbm, sem):
    copy = pltpu.make_async_copy(square_ref, square_hbm, sem)
    copy.start()
    multiply(s_ref, mk_ref, out_ref)
    copy.wait()


def add_parts(parts_ref):
    return (decode(parts_ref, 0) + decode(parts_ref, 1)) + (decode(parts_ref, 2) + decode(parts_ref, 3))


def finish_square(mask_ref, parts_ref, out_ref):
    total = add_parts(parts_ref)
    for t in range(2):
        rows = slice(t * BS, (t + 1) * BS)
        out_ref[rows, :] = (total[rows] * FACTOR * mask_ref[t * 8:t * 8 + 1, :]).astype(jnp.bfloat16)


def finish_sign(mask_ref, slab_ref, parts_ref, out_ref):
    total = add_parts(parts_ref)
    for t in range(2):
        rows = slice(t * BS, (t + 1) * BS)
        step = 1.5 * slab_ref[rows, :].astype(jnp.float32) - 0.5 * FACTOR * total[rows]
        out_ref[rows, :] = (step * mask_ref[t * 8:t * 8 + 1, :]).astype(jnp.bfloat16)


def shape(*dims, dtype=jnp.bfloat16):
    return jax.ShapeDtypeStruct(dims, dtype)


def kernel(body, n_in, out_shape, flops=0, moved=1 << 20):
    return pl.pallas_call(
        body,
        out_shape=out_shape,
        in_specs=vmem(n_in),
        out_specs=jax.tree.map(lambda _: pl.BlockSpec(memory_space=pltpu.VMEM), out_shape),
        compiler_params=pltpu.CompilerParams(vmem_limit_bytes=LIMIT),
        cost_estimate=pl.CostEstimate(flops=flops, bytes_accessed=moved, transcendentals=0),
    )


def local(values, occupancy):
    group = N_YL * N_X * N_YH
    anywhere = pl.BlockSpec(memory_space=pl.ANY)
    slab, mask, send = pl.pallas_call(
        prepare,
        out_shape=(shape(SLAB, BS), shape(16, BS, dtype=jnp.float32), shape(group, BS, BS)),
        in_specs=[anywhere, anywhere],
        out_specs=(anywhere, anywhere, anywhere),
        scratch_shapes=[
            pltpu.SMEM((3,), jnp.int32),
            pltpu.VMEM((3 * BS, BS), jnp.bfloat16),
            pltpu.VMEM((SLAB, BS), jnp.bfloat16),
            pltpu.VMEM((16, BS), jnp.float32),
            pltpu.VMEM((N_YH, BS, BS), jnp.bfloat16),
            pltpu.SemaphoreType.DMA((2,)),
            pltpu.SemaphoreType.DMA((2,)),
            pltpu.SemaphoreType.DMA((N_YL * N_X,)),
        ],
        compiler_params=pltpu.CompilerParams(vmem_limit_bytes=60 * 1024 * 1024),
    )(occupancy.reshape(3), values)
    mine = lax.all_to_all(send, ("yl", "x", "yh"), 0, 0, tiled=True)
    gathered = lax.all_gather(slab, "z", axis=1, tiled=True)
    mine, gathered = lax.optimization_barrier((mine, gathered))
    other = lax.ppermute(mine, "core", [(0, 1), (1, 0)])
    cost = dict(flops=2 * SLAB * 12 * BS * 4 * BS, moved=4 << 20)
    parts_shape = shape(N_YH, SLAB + N_GROUP, BS, dtype=jnp.int16)
    mk_shape = shape(N_Z * BS, N_YH * BS)
    parts, mk = kernel(first_product, 3, (parts_shape, mk_shape), **cost)(gathered, mine, other)
    parts = lax.all_to_all(parts, "yh", 0, 0, tiled=True, axis_index_groups=[PLACES])
    square = kernel(finish_square, 2, shape(SLAB, BS))(mask, parts)
    gathered = lax.all_gather(square, "z", axis=1, tiled=True)
    parts, square_slab = pl.pallas_call(
        second_product,
        out_shape=(parts_shape, shape(SLAB, BS)),
        in_specs=vmem(3),
        out_specs=(pl.BlockSpec(memory_space=pltpu.VMEM), anywhere),
        scratch_shapes=[pltpu.SemaphoreType.DMA],
        compiler_params=pltpu.CompilerParams(vmem_limit_bytes=LIMIT),
        cost_estimate=pl.CostEstimate(flops=cost["flops"], bytes_accessed=cost["moved"], transcendentals=0),
    )(gathered, mk, square)
    parts = lax.all_to_all(parts, "yh", 0, 0, tiled=True, axis_index_groups=[PLACES])
    sign_step = kernel(finish_sign, 3, shape(SLAB, BS))(mask, slab, parts)
    return (square_slab, sign_step)


def solution(mesh):
    fine = Mesh(
        mesh.devices.reshape(N_YL, N_X, N_CORE, N_Z, N_YH), ("yl", "x", "core", "z", "yh")
    )
    spec = P(("yl", "x", "core"), ("z", "yh"))
    return jax.shard_map(local, mesh=fine, in_specs=(spec, spec), out_specs=(spec, spec), check_vma=False)
```

```python
import math

import jax
import jax.numpy as jnp
from jax import lax
from jax.experimental import pallas as pl
from jax.experimental.pallas import tpu as pltpu
from jax.sharding import Mesh
from jax.sharding import PartitionSpec as P

BS = 128
SLAB = 256
ORDER = 6144
FACTOR = 1.0 / math.sqrt(ORDER)
N_YL, N_X, N_CORE, N_Z, N_YH = 2, 4, 2, 12, 4
N_GROUP = SLAB // 16
PLACES = [2, 3, 0, 1]
FIRST_PLACES = [3, 0, 1, 2]
SECOND_PLACES = [2, 3, 0, 1]
X_PLACES = [2, 3, 0, 1]
YL_PLACES = [0, 1]
LIMIT = 24 * 1024 * 1024


def vmem(n):
    return [pl.BlockSpec(memory_space=pltpu.VMEM)] * n


def row_index():
    return (lax.axis_index("yl") * N_X + lax.axis_index("x")) * N_CORE + lax.axis_index("core")


def prepare(
    occ_hbm, values_hbm, slab_hbm, mask_hbm, send_hbm,
    occ_ref, values_ref, slab_ref, mask_ref, blocks_ref, in_sem, out_sem, send_sem,
):
    read = [
        pltpu.make_async_copy(occ_hbm, occ_ref, in_sem.at[0]),
        pltpu.make_async_copy(values_hbm, values_ref, in_sem.at[1]),
    ]
    for copy in read:
        copy.start()
    for copy in read:
        copy.wait()
    written = []
    first = 3 * row_index()
    for q in range(N_YH):
        t = lax.rem(q + 4 * 48 - first, 4)
        held = jnp.minimum(t, 2)
        keep = jnp.where(t < 3, occ_ref[held], 0).astype(jnp.float32).astype(jnp.bfloat16)
        blocks_ref[PLACES.index(q)] = values_ref[pl.ds(pl.multiple_of(held * BS, BS), BS), :] * keep
    for j in range(N_YL * N_X):
        copy = pltpu.make_async_copy(blocks_ref, send_hbm.at[pl.ds(j * N_YH, N_YH)], send_sem.at[j])
        copy.start()
        written.append(copy)
    for t in range(2):
        rows = pl.ds(t * BS, BS)
        keep = occ_ref[t].astype(jnp.float32)
        slab_ref[rows, :] = values_ref[rows, :] * keep.astype(jnp.bfloat16)
        mask_ref[t * 8:(t + 1) * 8, :] = jnp.full((8, BS), keep, jnp.float32)
    for i, (source, target) in enumerate(((slab_ref, slab_hbm), (mask_ref, mask_hbm))):
        copy = pltpu.make_async_copy(source, target, out_sem.at[i])
        copy.start()
        written.append(copy)
    for copy in written:
        copy.wait()


def power_of_two(n, low):
    result = jnp.full(n.shape, 2.0**low, jnp.float32)
    for bit in range(7):
        factor = jnp.where(((n - low) >> bit) & 1 == 1, jnp.float32(2.0 ** (2**bit)), jnp.float32(1.0))
        result = result * factor
    return result


def encode(total):
    groups = total.reshape(N_GROUP, 16, BS)
    largest = jnp.max(jnp.abs(groups), axis=1)
    exponent = jnp.floor(jnp.log2(jnp.maximum(largest, 2.0**-100))).astype(jnp.int32) + 1
    scaled = groups * power_of_two(15 - exponent, -13)[:, None, :]
    rounded = jnp.clip(jnp.floor(scaled + 0.5), -32767.0, 32767.0).astype(jnp.int32)
    return rounded.reshape(SLAB, BS).astype(jnp.int16), exponent.astype(jnp.int16)


def decode(parts_ref, q):
    groups = parts_ref[q, :SLAB, :].astype(jnp.int32).astype(jnp.float32).reshape(N_GROUP, 16, BS)
    scale = power_of_two(parts_ref[q, SLAB:, :].astype(jnp.int32) - 15, -115)
    return (groups * scale[:, None, :]).reshape(SLAB, BS)


def multiply(s_ref, mk_ref, out_ref, places):
    total = jnp.dot(s_ref[...], mk_ref[...], preferred_element_type=jnp.float32)
    for q in range(N_YH):
        at = places.index(q)
        out_ref[at, :SLAB, :], out_ref[at, SLAB:, :] = encode(total[:, q * BS:(q + 1) * BS])


def place_of(chip):
    yl, x = lax.div(chip, N_X), lax.rem(chip, N_X)
    return lax.rem(yl + YL_PLACES[0], N_YL) * N_X + lax.rem(x + N_X - X_PLACES[0], N_X)


def first_product(s_ref, mine_ref, other_ref, out_ref, mk_ref):
    my_core, yh = lax.axis_index("core"), lax.axis_index("yh")
    for z in range(N_Z):
        r = lax.div(4 * z + yh, 3)
        slot = place_of(lax.div(r, 2)) * N_YH
        here = lax.rem(r, 2) == my_core

        @pl.when(here)
        def _():
            for q in range(N_YH):
                mk_ref[z * BS:(z + 1) * BS, q * BS:(q + 1) * BS] = mine_ref[slot + PLACES.index(q)]

        @pl.when(jnp.logical_not(here))
        def _():
            for q in range(N_YH):
                mk_ref[z * BS:(z + 1) * BS, q * BS:(q + 1) * BS] = other_ref[slot + PLACES.index(q)]

    multiply(s_ref, mk_ref, out_ref, FIRST_PLACES)


def second_product(s_ref, mk_ref, square_ref, out_ref, square_hbm, sem):
    copy = pltpu.make_async_copy(square_ref, square_hbm, sem)
    copy.start()
    multiply(s_ref, mk_ref, out_ref, SECOND_PLACES)
    copy.wait()


def add_parts(parts_ref):
    return (decode(parts_ref, 0) + decode(parts_ref, 1)) + (decode(parts_ref, 2) + decode(parts_ref, 3))


def finish_square(mask_ref, parts_ref, out_ref):
    total = add_parts(parts_ref)
    for t in range(2):
        rows = slice(t * BS, (t + 1) * BS)
        out_ref[rows, :] = (total[rows] * FACTOR * mask_ref[t * 8:t * 8 + 1, :]).astype(jnp.bfloat16)


def finish_sign(mask_ref, slab_ref, parts_ref, out_ref):
    total = add_parts(parts_ref)
    for t in range(2):
        rows = slice(t * BS, (t + 1) * BS)
        step = 1.5 * slab_ref[rows, :].astype(jnp.float32) - 0.5 * FACTOR * total[rows]
        out_ref[rows, :] = (step * mask_ref[t * 8:t * 8 + 1, :]).astype(jnp.bfloat16)


def shape(*dims, dtype=jnp.bfloat16):
    return jax.ShapeDtypeStruct(dims, dtype)


def kernel(body, n_in, out_shape, flops=0, moved=1 << 20):
    return pl.pallas_call(
        body,
        out_shape=out_shape,
        in_specs=vmem(n_in),
        out_specs=jax.tree.map(lambda _: pl.BlockSpec(memory_space=pltpu.VMEM), out_shape),
        compiler_params=pltpu.CompilerParams(vmem_limit_bytes=LIMIT),
        cost_estimate=pl.CostEstimate(flops=flops, bytes_accessed=moved, transcendentals=0),
    )


def local(values, occupancy):
    group = N_YL * N_X * N_YH
    order = [(yl * N_X + x) * N_YH + yh for yl in YL_PLACES for x in X_PLACES for yh in PLACES]
    anywhere = pl.BlockSpec(memory_space=pl.ANY)
    slab, mask, send = pl.pallas_call(
        prepare,
        out_shape=(shape(SLAB, BS), shape(16, BS, dtype=jnp.float32), shape(group, BS, BS)),
        in_specs=[anywhere, anywhere],
        out_specs=(anywhere, anywhere, anywhere),
        scratch_shapes=[
            pltpu.SMEM((3,), jnp.int32),
            pltpu.VMEM((3 * BS, BS), jnp.bfloat16),
            pltpu.VMEM((SLAB, BS), jnp.bfloat16),
            pltpu.VMEM((16, BS), jnp.float32),
            pltpu.VMEM((N_YH, BS, BS), jnp.bfloat16),
            pltpu.SemaphoreType.DMA((2,)),
            pltpu.SemaphoreType.DMA((2,)),
            pltpu.SemaphoreType.DMA((N_YL * N_X,)),
        ],
        compiler_params=pltpu.CompilerParams(vmem_limit_bytes=60 * 1024 * 1024),
    )(occupancy.reshape(3), values)
    mine = lax.all_to_all(send, ("yl", "x", "yh"), 0, 0, tiled=True, axis_index_groups=[order])
    gathered = lax.all_gather(slab, "z", axis=1, tiled=True)
    mine, gathered = lax.optimization_barrier((mine, gathered))
    other = lax.ppermute(mine, "core", [(0, 1), (1, 0)])
    cost = dict(flops=2 * SLAB * 12 * BS * 4 * BS, moved=4 << 20)
    parts_shape = shape(N_YH, SLAB + N_GROUP, BS, dtype=jnp.int16)
    mk_shape = shape(N_Z * BS, N_YH * BS)
    parts, mk = kernel(first_product, 3, (parts_shape, mk_shape), **cost)(gathered, mine, other)
    parts = lax.all_to_all(parts, "yh", 0, 0, tiled=True, axis_index_groups=[FIRST_PLACES])
    square = kernel(finish_square, 2, shape(SLAB, BS))(mask, parts)
    gathered = lax.all_gather(square, "z", axis=1, tiled=True)
    parts, square_slab = pl.pallas_call(
        second_product,
        out_shape=(parts_shape, shape(SLAB, BS)),
        in_specs=vmem(3),
        out_specs=(pl.BlockSpec(memory_space=pltpu.VMEM), anywhere),
        scratch_shapes=[pltpu.SemaphoreType.DMA],
        compiler_params=pltpu.CompilerParams(vmem_limit_bytes=LIMIT),
        cost_estimate=pl.CostEstimate(flops=cost["flops"], bytes_accessed=cost["moved"], transcendentals=0),
    )(gathered, mk, square)
    parts = lax.all_to_all(parts, "yh", 0, 0, tiled=True, axis_index_groups=[SECOND_PLACES])
    sign_step = kernel(finish_sign, 3, shape(SLAB, BS))(mask, slab, parts)
    return (square_slab, sign_step)


def solution(mesh):
    fine = Mesh(
        mesh.devices.reshape(N_YL, N_X, N_CORE, N_Z, N_YH), ("yl", "x", "core", "z", "yh")
    )
    spec = P(("yl", "x", "core"), ("z", "yh"))
    return jax.shard_map(local, mesh=fine, in_specs=(spec, spec), out_specs=(spec, spec), check_vma=False)
```

```python
import math

import jax
import jax.numpy as jnp
from jax import lax
from jax.experimental import pallas as pl
from jax.experimental.pallas import tpu as pltpu
from jax.sharding import Mesh
from jax.sharding import PartitionSpec as P

BS = 128
SLAB = 256
ORDER = 6144
FACTOR = 1.0 / math.sqrt(ORDER)
N_YL, N_X, N_CORE, N_Z, N_YH = 2, 4, 2, 12, 4
N_GROUP = SLAB // 16
PLACES = [2, 3, 0, 1]
FIRST_PLACES = [3, 0, 1, 2]
SECOND_PLACES = [2, 3, 0, 1]
X_PLACES = [1, 2, 3, 0]
YL_PLACES = [0, 1]
LIMIT = 24 * 1024 * 1024


def vmem(n):
    return [pl.BlockSpec(memory_space=pltpu.VMEM)] * n


def row_index():
    return (lax.axis_index("yl") * N_X + lax.axis_index("x")) * N_CORE + lax.axis_index("core")


def prepare(
    occ_hbm, values_hbm, slab_hbm, mask_hbm, send_hbm,
    occ_ref, values_ref, slab_ref, mask_ref, blocks_ref, in_sem, out_sem, send_sem,
):
    read = [
        pltpu.make_async_copy(occ_hbm, occ_ref, in_sem.at[0]),
        pltpu.make_async_copy(values_hbm, values_ref, in_sem.at[1]),
    ]
    for copy in read:
        copy.start()
    for copy in read:
        copy.wait()
    written = []
    first = 3 * row_index()
    for q in range(N_YH):
        t = lax.rem(q + 4 * 48 - first, 4)
        held = jnp.minimum(t, 2)
        keep = jnp.where(t < 3, occ_ref[held], 0).astype(jnp.float32).astype(jnp.bfloat16)
        blocks_ref[PLACES.index(q)] = values_ref[pl.ds(pl.multiple_of(held * BS, BS), BS), :] * keep
    for j in range(N_YL * N_X):
        copy = pltpu.make_async_copy(blocks_ref, send_hbm.at[pl.ds(j * N_YH, N_YH)], send_sem.at[j])
        copy.start()
        written.append(copy)
    for t in range(2):
        rows = pl.ds(t * BS, BS)
        keep = occ_ref[t].astype(jnp.float32)
        slab_ref[rows, :] = values_ref[rows, :] * keep.astype(jnp.bfloat16)
        mask_ref[t * 8:(t + 1) * 8, :] = jnp.full((8, BS), keep, jnp.float32)
    for i, (source, target) in enumerate(((slab_ref, slab_hbm), (mask_ref, mask_hbm))):
        copy = pltpu.make_async_copy(source, target, out_sem.at[i])
        copy.start()
        written.append(copy)
    for copy in written:
        copy.wait()


def power_of_two(n, low):
    result = jnp.full(n.shape, 2.0**low, jnp.float32)
    for bit in range(7):
        factor = jnp.where(((n - low) >> bit) & 1 == 1, jnp.float32(2.0 ** (2**bit)), jnp.float32(1.0))
        result = result * factor
    return result


def encode(total):
    groups = total.reshape(N_GROUP, 16, BS)
    largest = jnp.max(jnp.abs(groups), axis=1)
    exponent = jnp.floor(jnp.log2(jnp.maximum(largest, 2.0**-100))).astype(jnp.int32) + 1
    scaled = groups * power_of_two(15 - exponent, -13)[:, None, :]
    rounded = jnp.clip(jnp.floor(scaled + 0.5), -32767.0, 32767.0).astype(jnp.int32)
    return rounded.reshape(SLAB, BS).astype(jnp.int16), exponent.astype(jnp.int16)


def decode(parts_ref, q):
    groups = parts_ref[q, :SLAB, :].astype(jnp.int32).astype(jnp.float32).reshape(N_GROUP, 16, BS)
    scale = power_of_two(parts_ref[q, SLAB:, :].astype(jnp.int32) - 15, -115)
    return (groups * scale[:, None, :]).reshape(SLAB, BS)


def multiply(s_ref, mk_ref, out_ref, places):
    total = jnp.dot(s_ref[...], mk_ref[...], preferred_element_type=jnp.float32)
    for q in range(N_YH):
        at = places.index(q)
        out_ref[at, :SLAB, :], out_ref[at, SLAB:, :] = encode(total[:, q * BS:(q + 1) * BS])


def place_of(chip):
    yl, x = lax.div(chip, N_X), lax.rem(chip, N_X)
    return lax.rem(yl + YL_PLACES[0], N_YL) * N_X + lax.rem(x + N_X - X_PLACES[0], N_X)


def first_product(s_ref, mine_ref, other_ref, out_ref, mk_ref):
    my_core, yh = lax.axis_index("core"), lax.axis_index("yh")
    for z in range(N_Z):
        r = lax.div(4 * z + yh, 3)
        slot = place_of(lax.div(r, 2)) * N_YH
        here = lax.rem(r, 2) == my_core

        @pl.when(here)
        def _():
            for q in range(N_YH):
                mk_ref[z * BS:(z + 1) * BS, q * BS:(q + 1) * BS] = mine_ref[slot + PLACES.index(q)]

        @pl.when(jnp.logical_not(here))
        def _():
            for q in range(N_YH):
                mk_ref[z * BS:(z + 1) * BS, q * BS:(q + 1) * BS] = other_ref[slot + PLACES.index(q)]

    multiply(s_ref, mk_ref, out_ref, FIRST_PLACES)


def second_product(s_ref, mk_ref, square_ref, out_ref, square_hbm, sem):
    copy = pltpu.make_async_copy(square_ref, square_hbm, sem)
    copy.start()
    multiply(s_ref, mk_ref, out_ref, SECOND_PLACES)
    copy.wait()


def add_parts(parts_ref):
    return (decode(parts_ref, 0) + decode(parts_ref, 1)) + (decode(parts_ref, 2) + decode(parts_ref, 3))


def finish_square(mask_ref, parts_ref, out_ref):
    total = add_parts(parts_ref)
    for t in range(2):
        rows = slice(t * BS, (t + 1) * BS)
        out_ref[rows, :] = (total[rows] * FACTOR * mask_ref[t * 8:t * 8 + 1, :]).astype(jnp.bfloat16)


def finish_sign(mask_ref, slab_ref, parts_ref, out_ref):
    total = add_parts(parts_ref)
    for t in range(2):
        rows = slice(t * BS, (t + 1) * BS)
        step = 1.5 * slab_ref[rows, :].astype(jnp.float32) - 0.5 * FACTOR * total[rows]
        out_ref[rows, :] = (step * mask_ref[t * 8:t * 8 + 1, :]).astype(jnp.bfloat16)


def shape(*dims, dtype=jnp.bfloat16):
    return jax.ShapeDtypeStruct(dims, dtype)


def kernel(body, n_in, out_shape, flops=0, moved=1 << 20):
    return pl.pallas_call(
        body,
        out_shape=out_shape,
        in_specs=vmem(n_in),
        out_specs=jax.tree.map(lambda _: pl.BlockSpec(memory_space=pltpu.VMEM), out_shape),
        compiler_params=pltpu.CompilerParams(vmem_limit_bytes=LIMIT),
        cost_estimate=pl.CostEstimate(flops=flops, bytes_accessed=moved, transcendentals=0),
    )


def local(values, occupancy):
    group = N_YL * N_X * N_YH
    order = [(yl * N_X + x) * N_YH + yh for yl in YL_PLACES for x in X_PLACES for yh in PLACES]
    anywhere = pl.BlockSpec(memory_space=pl.ANY)
    slab, mask, send = pl.pallas_call(
        prepare,
        out_shape=(shape(SLAB, BS), shape(16, BS, dtype=jnp.float32), shape(group, BS, BS)),
        in_specs=[anywhere, anywhere],
        out_specs=(anywhere, anywhere, anywhere),
        scratch_shapes=[
            pltpu.SMEM((3,), jnp.int32),
            pltpu.VMEM((3 * BS, BS), jnp.bfloat16),
            pltpu.VMEM((SLAB, BS), jnp.bfloat16),
            pltpu.VMEM((16, BS), jnp.float32),
            pltpu.VMEM((N_YH, BS, BS), jnp.bfloat16),
            pltpu.SemaphoreType.DMA((2,)),
            pltpu.SemaphoreType.DMA((2,)),
            pltpu.SemaphoreType.DMA((N_YL * N_X,)),
        ],
        compiler_params=pltpu.CompilerParams(vmem_limit_bytes=60 * 1024 * 1024),
    )(occupancy.reshape(3), values)
    mine = lax.all_to_all(send, ("yl", "x", "yh"), 0, 0, tiled=True, axis_index_groups=[order])
    gathered = lax.all_gather(slab, "z", axis=1, tiled=True)
    mine, gathered = lax.optimization_barrier((mine, gathered))
    other = lax.ppermute(mine, "core", [(0, 1), (1, 0)])
    cost = dict(flops=2 * SLAB * 12 * BS * 4 * BS, moved=4 << 20)
    parts_shape = shape(N_YH, SLAB + N_GROUP, BS, dtype=jnp.int16)
    mk_shape = shape(N_Z * BS, N_YH * BS)
    parts, mk = kernel(first_product, 3, (parts_shape, mk_shape), **cost)(gathered, mine, other)
    parts = lax.all_to_all(parts, "yh", 0, 0, tiled=True, axis_index_groups=[FIRST_PLACES])
    square = kernel(finish_square, 2, shape(SLAB, BS))(mask, parts)
    gathered = lax.all_gather(square, "z", axis=1, tiled=True)
    parts, square_slab = pl.pallas_call(
        second_product,
        out_shape=(parts_shape, shape(SLAB, BS)),
        in_specs=vmem(3),
        out_specs=(pl.BlockSpec(memory_space=pltpu.VMEM), anywhere),
        scratch_shapes=[pltpu.SemaphoreType.DMA],
        compiler_params=pltpu.CompilerParams(vmem_limit_bytes=LIMIT),
        cost_estimate=pl.CostEstimate(flops=cost["flops"], bytes_accessed=cost["moved"], transcendentals=0),
    )(gathered, mk, square)
    parts = lax.all_to_all(parts, "yh", 0, 0, tiled=True, axis_index_groups=[SECOND_PLACES])
    sign_step = kernel(finish_sign, 3, shape(SLAB, BS))(mask, slab, parts)
    return (square_slab, sign_step)


def solution(mesh):
    fine = Mesh(
        mesh.devices.reshape(N_YL, N_X, N_CORE, N_Z, N_YH), ("yl", "x", "core", "z", "yh")
    )
    spec = P(("yl", "x", "core"), ("z", "yh"))
    return jax.shard_map(local, mesh=fine, in_specs=(spec, spec), out_specs=(spec, spec), check_vma=False)
```

```python
import math

import jax
import jax.numpy as jnp
from jax import lax
from jax.experimental import pallas as pl
from jax.experimental.pallas import tpu as pltpu
from jax.sharding import Mesh
from jax.sharding import PartitionSpec as P

BS = 128
SLAB = 256
ORDER = 6144
FACTOR = 1.0 / math.sqrt(ORDER)
N_YL, N_X, N_CORE, N_Z, N_YH = 2, 4, 2, 12, 4
N_GROUP = SLAB // 16
PLACES = [2, 3, 0, 1]
FIRST_PLACES = [3, 0, 1, 2]
SECOND_PLACES = [2, 3, 0, 1]
X_PLACES = [2, 3, 0, 1]
YL_PLACES = [1, 0]
LIMIT = 24 * 1024 * 1024


def vmem(n):
    return [pl.BlockSpec(memory_space=pltpu.VMEM)] * n


def row_index():
    return (lax.axis_index("yl") * N_X + lax.axis_index("x")) * N_CORE + lax.axis_index("core")


def prepare(
    occ_hbm, values_hbm, slab_hbm, mask_hbm, send_hbm,
    occ_ref, values_ref, slab_ref, mask_ref, blocks_ref, in_sem, out_sem, send_sem,
):
    read = [
        pltpu.make_async_copy(occ_hbm, occ_ref, in_sem.at[0]),
        pltpu.make_async_copy(values_hbm, values_ref, in_sem.at[1]),
    ]
    for copy in read:
        copy.start()
    for copy in read:
        copy.wait()
    written = []
    first = 3 * row_index()
    for q in range(N_YH):
        t = lax.rem(q + 4 * 48 - first, 4)
        held = jnp.minimum(t, 2)
        keep = jnp.where(t < 3, occ_ref[held], 0).astype(jnp.float32).astype(jnp.bfloat16)
        blocks_ref[PLACES.index(q)] = values_ref[pl.ds(pl.multiple_of(held * BS, BS), BS), :] * keep
    for j in range(N_YL * N_X):
        copy = pltpu.make_async_copy(blocks_ref, send_hbm.at[pl.ds(j * N_YH, N_YH)], send_sem.at[j])
        copy.start()
        written.append(copy)
    for t in range(2):
        rows = pl.ds(t * BS, BS)
        keep = occ_ref[t].astype(jnp.float32)
        slab_ref[rows, :] = values_ref[rows, :] * keep.astype(jnp.bfloat16)
        mask_ref[t * 8:(t + 1) * 8, :] = jnp.full((8, BS), keep, jnp.float32)
    for i, (source, target) in enumerate(((slab_ref, slab_hbm), (mask_ref, mask_hbm))):
        copy = pltpu.make_async_copy(source, target, out_sem.at[i])
        copy.start()
        written.append(copy)
    for copy in written:
        copy.wait()


def power_of_two(n, low):
    result = jnp.full(n.shape, 2.0**low, jnp.float32)
    for bit in range(7):
        factor = jnp.where(((n - low) >> bit) & 1 == 1, jnp.float32(2.0 ** (2**bit)), jnp.float32(1.0))
        result = result * factor
    return result


def encode(total):
    groups = total.reshape(N_GROUP, 16, BS)
    largest = jnp.max(jnp.abs(groups), axis=1)
    exponent = jnp.floor(jnp.log2(jnp.maximum(largest, 2.0**-100))).astype(jnp.int32) + 1
    scaled = groups * power_of_two(15 - exponent, -13)[:, None, :]
    rounded = jnp.clip(jnp.floor(scaled + 0.5), -32767.0, 32767.0).astype(jnp.int32)
    return rounded.reshape(SLAB, BS).astype(jnp.int16), exponent.astype(jnp.int16)


def decode(parts_ref, q):
    groups = parts_ref[q, :SLAB, :].astype(jnp.int32).astype(jnp.float32).reshape(N_GROUP, 16, BS)
    scale = power_of_two(parts_ref[q, SLAB:, :].astype(jnp.int32) - 15, -115)
    return (groups * scale[:, None, :]).reshape(SLAB, BS)


def multiply(s_ref, mk_ref, out_ref, places):
    total = jnp.dot(s_ref[...], mk_ref[...], preferred_element_type=jnp.float32)
    for q in range(N_YH):
        at = places.index(q)
        out_ref[at, :SLAB, :], out_ref[at, SLAB:, :] = encode(total[:, q * BS:(q + 1) * BS])


def place_of(chip):
    yl, x = lax.div(chip, N_X), lax.rem(chip, N_X)
    return lax.rem(yl + YL_PLACES[0], N_YL) * N_X + lax.rem(x + N_X - X_PLACES[0], N_X)


def first_product(s_ref, mine_ref, other_ref, out_ref, mk_ref):
    my_core, yh = lax.axis_index("core"), lax.axis_index("yh")
    for z in range(N_Z):
        r = lax.div(4 * z + yh, 3)
        slot = place_of(lax.div(r, 2)) * N_YH
        here = lax.rem(r, 2) == my_core

        @pl.when(here)
        def _():
            for q in range(N_YH):
                mk_ref[z * BS:(z + 1) * BS, q * BS:(q + 1) * BS] = mine_ref[slot + PLACES.index(q)]

        @pl.when(jnp.logical_not(here))
        def _():
            for q in range(N_YH):
                mk_ref[z * BS:(z + 1) * BS, q * BS:(q + 1) * BS] = other_ref[slot + PLACES.index(q)]

    multiply(s_ref, mk_ref, out_ref, FIRST_PLACES)


def second_product(s_ref, mk_ref, square_ref, out_ref, square_hbm, sem):
    copy = pltpu.make_async_copy(square_ref, square_hbm, sem)
    copy.start()
    multiply(s_ref, mk_ref, out_ref, SECOND_PLACES)
    copy.wait()


def add_parts(parts_ref):
    return (decode(parts_ref, 0) + decode(parts_ref, 1)) + (decode(parts_ref, 2) + decode(parts_ref, 3))


def finish_square(mask_ref, parts_ref, out_ref):
    total = add_parts(parts_ref)
    for t in range(2):
        rows = slice(t * BS, (t + 1) * BS)
        out_ref[rows, :] = (total[rows] * FACTOR * mask_ref[t * 8:t * 8 + 1, :]).astype(jnp.bfloat16)


def finish_sign(mask_ref, slab_ref, parts_ref, out_ref):
    total = add_parts(parts_ref)
    for t in range(2):
        rows = slice(t * BS, (t + 1) * BS)
        step = 1.5 * slab_ref[rows, :].astype(jnp.float32) - 0.5 * FACTOR * total[rows]
        out_ref[rows, :] = (step * mask_ref[t * 8:t * 8 + 1, :]).astype(jnp.bfloat16)


def shape(*dims, dtype=jnp.bfloat16):
    return jax.ShapeDtypeStruct(dims, dtype)


def kernel(body, n_in, out_shape, flops=0, moved=1 << 20):
    return pl.pallas_call(
        body,
        out_shape=out_shape,
        in_specs=vmem(n_in),
        out_specs=jax.tree.map(lambda _: pl.BlockSpec(memory_space=pltpu.VMEM), out_shape),
        compiler_params=pltpu.CompilerParams(vmem_limit_bytes=LIMIT),
        cost_estimate=pl.CostEstimate(flops=flops, bytes_accessed=moved, transcendentals=0),
    )


def local(values, occupancy):
    group = N_YL * N_X * N_YH
    order = [(yl * N_X + x) * N_YH + yh for yl in YL_PLACES for x in X_PLACES for yh in PLACES]
    anywhere = pl.BlockSpec(memory_space=pl.ANY)
    slab, mask, send = pl.pallas_call(
        prepare,
        out_shape=(shape(SLAB, BS), shape(16, BS, dtype=jnp.float32), shape(group, BS, BS)),
        in_specs=[anywhere, anywhere],
        out_specs=(anywhere, anywhere, anywhere),
        scratch_shapes=[
            pltpu.SMEM((3,), jnp.int32),
            pltpu.VMEM((3 * BS, BS), jnp.bfloat16),
            pltpu.VMEM((SLAB, BS), jnp.bfloat16),
            pltpu.VMEM((16, BS), jnp.float32),
            pltpu.VMEM((N_YH, BS, BS), jnp.bfloat16),
            pltpu.SemaphoreType.DMA((2,)),
            pltpu.SemaphoreType.DMA((2,)),
            pltpu.SemaphoreType.DMA((N_YL * N_X,)),
        ],
        compiler_params=pltpu.CompilerParams(vmem_limit_bytes=60 * 1024 * 1024),
    )(occupancy.reshape(3), values)
    mine = lax.all_to_all(send, ("yl", "x", "yh"), 0, 0, tiled=True, axis_index_groups=[order])
    gathered = lax.all_gather(slab, "z", axis=1, tiled=True)
    mine, gathered = lax.optimization_barrier((mine, gathered))
    other = lax.ppermute(mine, "core", [(0, 1), (1, 0)])
    cost = dict(flops=2 * SLAB * 12 * BS * 4 * BS, moved=4 << 20)
    parts_shape = shape(N_YH, SLAB + N_GROUP, BS, dtype=jnp.int16)
    mk_shape = shape(N_Z * BS, N_YH * BS)
    parts, mk = kernel(first_product, 3, (parts_shape, mk_shape), **cost)(gathered, mine, other)
    parts = lax.all_to_all(parts, "yh", 0, 0, tiled=True, axis_index_groups=[FIRST_PLACES])
    square = kernel(finish_square, 2, shape(SLAB, BS))(mask, parts)
    gathered = lax.all_gather(square, "z", axis=1, tiled=True)
    parts, square_slab = pl.pallas_call(
        second_product,
        out_shape=(parts_shape, shape(SLAB, BS)),
        in_specs=vmem(3),
        out_specs=(pl.BlockSpec(memory_space=pltpu.VMEM), anywhere),
        scratch_shapes=[pltpu.SemaphoreType.DMA],
        compiler_params=pltpu.CompilerParams(vmem_limit_bytes=LIMIT),
        cost_estimate=pl.CostEstimate(flops=cost["flops"], bytes_accessed=cost["moved"], transcendentals=0),
    )(gathered, mk, square)
    parts = lax.all_to_all(parts, "yh", 0, 0, tiled=True, axis_index_groups=[SECOND_PLACES])
    sign_step = kernel(finish_sign, 3, shape(SLAB, BS))(mask, slab, parts)
    return (square_slab, sign_step)


def solution(mesh):
    fine = Mesh(
        mesh.devices.reshape(N_YL, N_X, N_CORE, N_Z, N_YH), ("yl", "x", "core", "z", "yh")
    )
    spec = P(("yl", "x", "core"), ("z", "yh"))
    return jax.shard_map(local, mesh=fine, in_specs=(spec, spec), out_specs=(spec, spec), check_vma=False)
```
